32 devices in a mesh: row: 4 (over y, x), col: 8 (over z, core).
Axes of the slice: x: 2, y: 2, z: 4, core: 2. Of those that a mesh axis runs over, the one named last changes fastest.
Arguments:
- features: bfloat16 [8192, 128], P(('row', 'col')), may hold values from -6 to 6
- tiles: bfloat16 [4, 8, 48, 128, 128], P('row', 'col'), may hold values from 0 to 1.5, as said below
- tile_row: int32 [4, 8, 48], P('row', 'col'), may hold values from 0 to 15, as said below
- tile_col: int32 [4, 8, 48], P('row', 'col'), may hold values from 0 to 7, as said below
- tile_live: int32 [4, 8], P('row', 'col'), may hold values from 1 to 48, as said below
- w_first: bfloat16 [128, 256], replicated, may hold values from -0.5 to 0.5
- b_first: float32 [256], replicated, may hold values from -3 to 3
- w_second: bfloat16 [256, 172], replicated, may hold values from -0.375 to 0.375
- b_second: float32 [172], replicated, may hold values from -3 to 3
- grad_logits: bfloat16 [8192, 172], P(('row', 'col')), may hold values from -0.039794922 to 0.039794922
Outputs:
- logits: bfloat16 [8192, 172], P(('row', 'col'))
- grad_w1: float32 [128, 256], replicated
- grad_b1: float32 [256], replicated
- grad_w2: float32 [256, 172], replicated
- grad_b2: float32 [172], replicated
The draws below stay inside these ranges and needn't reach their ends.
Inputs may be any that keep to these rules, and one draw needn't show every extreme that they name: `tiles`: each entry is zero (no edge) or an edge weight. `tile_row`: block rows are local to a device's grid row, below 2 * 8. `tile_col`: block columns are local to a device's grid column, below 2 * 4; the occupied slots of one device name distinct (row, column) pairs. Slots from tile_live onward are unused: whatever their tiles and indices hold is ignored. Some device has all 48 slots occupied.
All inputs are finite; a program needn't handle non-finite values.
Results may differ from the reference program's by a relative error of at most 0.0051.
Values may be sent and summed in bfloat16 or wider, within the bound.
No kernel may reach another device: no remote copies, remote signals or barrier semaphores. Data moves between devices by JAX's collectives and lax.ppermute only.
A program may use at most 64 MiB of HBM per device.

```python
import jax
import jax.numpy as jnp
from jax import lax

FIN = 128
HID = 256
CLS = 172
BS = 128
BPD = 2
NODES = 8192
TPD = 48
N_ROW = 4
N_COL = 8


def pick_positions(key):
    total = BPD * BPD * N_ROW * N_COL
    keys = jax.random.split(key, N_ROW * N_COL)
    chosen = jax.vmap(lambda single: jax.random.permutation(single, total)[:TPD])(keys)
    return chosen.reshape(N_ROW, N_COL, TPD).astype(jnp.int32)


def draw_tiles(key, part):
    key = jax.random.fold_in(key, 11)
    value_key, edge_key = jax.random.split(key)
    shape = (N_ROW, N_COL, TPD, BS, BS)
    values = jax.random.uniform(value_key, shape, jnp.float32, 0.5, 1.5)
    edges = (jax.random.randint(edge_key, shape, 0, BS * N_COL // 2) == 0).astype(jnp.float32)
    return (values * edges).astype(jnp.bfloat16)


def draw_tile_row(key, part):
    return (pick_positions(key) // (BPD * N_ROW)).astype(jnp.int32)


def draw_tile_col(key, part):
    return (pick_positions(key) % (BPD * N_ROW)).astype(jnp.int32)


def draw_tile_live(key, part):
    key = jax.random.fold_in(key, 7)
    first_key, second_key = jax.random.split(key)
    raw = jax.random.randint(first_key, (N_ROW * N_COL,), 1, TPD + 1)
    counts = jnp.maximum(1, (raw * raw + raw * TPD) // (2 * TPD))
    busiest = jax.random.randint(second_key, (), 0, N_ROW * N_COL)
    counts = counts.at[busiest].set(TPD)
    return counts.reshape(N_ROW, N_COL).astype(jnp.int32)


def block_scale(own_key, shape, pieces, low, largest):
    loudness = 1.0
    for axis_at, parts in pieces:
        steps = jax.random.uniform(jax.random.fold_in(jax.random.fold_in(own_key, 6), axis_at), (parts,), jnp.float32, low / len(pieces), largest / len(pieces))
        loudness = loudness * jnp.repeat(jnp.exp(steps), shape[axis_at] // parts).reshape((-1,) + (1,) * (len(shape) - 1 - axis_at))
    return loudness


def bell_draw(key, shape, scale, limit, cuts=(), held_as=jnp.bfloat16):
    entries = jax.random.normal(key, shape, jnp.float32) * scale
    if len(cuts) > 0:
        entries = block_scale(key, shape, cuts, -0.22, 0.18) * entries
    return jnp.clip(entries, min=-limit, max=limit).astype(held_as)


def setup_inputs(seed: int = 0) -> dict:
    key_of = jax.random.split(jax.random.key(seed), 11)
    features = bell_draw(key_of[0], (NODES, FIN), 1.0, 6.0, ((0, 32),))
    tiles = draw_tiles(jax.random.fold_in(key_of[10], 71), 0)
    tile_row = draw_tile_row(jax.random.fold_in(key_of[10], 71), 0)
    tile_col = draw_tile_col(jax.random.fold_in(key_of[10], 71), 0)
    tile_live = draw_tile_live(jax.random.fold_in(key_of[10], 71), 0)
    w_first = bell_draw(key_of[5], (FIN, HID), FIN ** -0.5, 0.5)
    b_first = bell_draw(key_of[6], (HID,), 0.5, 3.0, (), jnp.float32)
    w_second = bell_draw(key_of[7], (HID, CLS), HID ** -0.5, 0.375)
    b_second = bell_draw(key_of[8], (CLS,), 0.5, 3.0, (), jnp.float32)
    grad_logits = bell_draw(key_of[9], (NODES, CLS), 0.005, 0.039794922, ((0, 32),))
    return dict(features=features, tiles=tiles, tile_row=tile_row, tile_col=tile_col, tile_live=tile_live, w_first=w_first, b_first=b_first, w_second=w_second, b_second=b_second, grad_logits=grad_logits)


def activation(values):
    return jax.nn.gelu(values, approximate=True)

def block_sums(tiles, tile_row, tile_col, tile_live, source, width, transpose):
    tile_all = tiles.reshape(N_ROW * N_COL, TPD, BS, BS)
    rows_all = tile_row.reshape(N_ROW * N_COL, TPD).astype(jnp.int32)
    cols_all = tile_col.reshape(N_ROW * N_COL, TPD).astype(jnp.int32)
    live_all = tile_live.reshape(N_ROW * N_COL).astype(jnp.int32)
    number = jnp.arange(N_ROW * N_COL, dtype=jnp.int32)
    if transpose:
        source_rows = source.reshape(N_ROW, N_COL * BPD, BS, width)
        start_acc = jnp.zeros((N_ROW, N_COL, BPD, BS, width), jnp.float32)
    else:
        source_cols = source.reshape(N_ROW, N_COL, BPD, BS, width)
        start_acc = jnp.zeros((N_ROW, N_COL * BPD, BS, width), jnp.float32)

    def visit(total, items):
        tile_dev, rows_dev, cols_dev, live_count, device = items
        grid_row = device // N_COL
        grid_col = device % N_COL
        live_mask = (jnp.arange(TPD, dtype=jnp.int32) < live_count).astype(jnp.float32)
        tile_float = tile_dev.astype(jnp.float32)
        if transpose:
            blocks = lax.dynamic_index_in_dim(source_rows, grid_row, 0, keepdims=False)
            picked = blocks[rows_dev].astype(jnp.float32)
            product = jnp.einsum('tij,tif->tjf', tile_float, picked, precision=lax.Precision.HIGHEST)
            product = product * live_mask[:, None, None]
            partial_value = jax.ops.segment_sum(product, cols_dev, num_segments=N_ROW * BPD)
            partial_value = partial_value.reshape(N_ROW, BPD, BS, width)
            return (total.at[:, grid_col].add(partial_value), None)
        blocks = lax.dynamic_index_in_dim(source_cols, grid_col, 1, keepdims=False)
        blocks = blocks.reshape(N_ROW * BPD, BS, width)
        picked = blocks[cols_dev].astype(jnp.float32)
        product = jnp.einsum('tij,tjf->tif', tile_float, picked, precision=lax.Precision.HIGHEST)
        product = product * live_mask[:, None, None]
        partial_value = jax.ops.segment_sum(product, rows_dev, num_segments=N_COL * BPD)
        return (total.at[grid_row].add(partial_value), None)
    total, _ = lax.scan(visit, start_acc, (tile_all, rows_all, cols_all, live_all, number))
    return total.reshape(NODES, width)

def degrees(tiles, tile_row, tile_live):
    tile_all = tiles.reshape(N_ROW * N_COL, TPD, BS, BS)
    rows_all = tile_row.reshape(N_ROW * N_COL, TPD).astype(jnp.int32)
    live_all = tile_live.reshape(N_ROW * N_COL).astype(jnp.int32)
    number = jnp.arange(N_ROW * N_COL, dtype=jnp.int32)

    def visit(total, items):
        tile_dev, rows_dev, live_count, device = items
        grid_row = device // N_COL
        live_mask = (jnp.arange(TPD, dtype=jnp.int32) < live_count).astype(jnp.float32)
        sums = lax.optimization_barrier(jnp.sum(tile_dev.astype(jnp.float32), axis=2)) * live_mask[:, None]
        partial_value = jax.ops.segment_sum(sums, rows_dev, num_segments=N_COL * BPD)
        return (total.at[grid_row].add(partial_value), None)
    start_acc = jnp.zeros((N_ROW, N_COL * BPD, BS), jnp.float32)
    total, _ = lax.scan(visit, start_acc, (tile_all, rows_all, live_all, number))
    return 1.0 + total.reshape(NODES)

def reference(features, tiles, tile_row, tile_col, tile_live, w_first, b_first, w_second, b_second, grad_logits):
    highest = lax.Precision.HIGHEST
    deg = degrees(tiles, tile_row, tile_live)
    first_sum = block_sums(tiles, tile_row, tile_col, tile_live, features, FIN, False)
    agg1 = ((first_sum + features.astype(jnp.float32)) / deg[:, None]).astype(jnp.bfloat16)
    z1 = jnp.dot(agg1, w_first, preferred_element_type=jnp.float32) + b_first
    h1 = activation(z1).astype(jnp.bfloat16)
    second_sum = block_sums(tiles, tile_row, tile_col, tile_live, h1, HID, False)
    agg2 = (second_sum + h1.astype(jnp.float32)) / deg[:, None]
    w_second_float = w_second.astype(jnp.float32)
    logits = (jnp.dot(agg2, w_second_float, precision=highest) + b_second).astype(jnp.bfloat16)
    scaled = (grad_logits.astype(jnp.float32) / deg[:, None]).astype(jnp.bfloat16)
    back_sum = block_sums(tiles, tile_row, tile_col, tile_live, scaled, CLS, True)
    q_field = back_sum + scaled.astype(jnp.float32)
    grad_w2 = jnp.dot(h1.astype(jnp.float32).T, q_field, precision=highest)
    grad_b2 = lax.optimization_barrier(jnp.sum(grad_logits.astype(jnp.float32), axis=0))
    d_hidden = jnp.dot(q_field, w_second_float.T, precision=highest)
    d_z1 = jax.vjp(activation, z1)[1](d_hidden)[0]
    d_half = d_z1.astype(jnp.bfloat16)
    grad_w1 = jnp.dot(agg1.T, d_half, preferred_element_type=jnp.float32)
    grad_b1 = lax.optimization_barrier(jnp.sum(d_z1, axis=0))
    return (logits, grad_w1, grad_b1, grad_w2, grad_b2)
```

```python
import functools

import jax
import jax.numpy as jnp
from jax import lax
from jax.experimental import pallas as pl
from jax.experimental.pallas import tpu as pltpu
from jax.sharding import PartitionSpec as P

BF16 = jnp.bfloat16
F32 = jnp.float32


def exchange(value, axis, mask):
    count = lax.axis_size(axis)
    return lax.ppermute(value, axis, [(i, i ^ mask) for i in range(count)])


def swap_halves(value, parts):
    pairs = value.reshape((parts, 2, -1) + value.shape[1:])
    return jnp.concatenate([pairs[:, 1:], pairs[:, :1]], axis=1).reshape(value.shape)


def dense_kernel(own, row_ref, col_ref, live_ref, place_ref, tiles_ref, dense_ref, degree_ref):
    slots, block, _ = tiles_ref.shape
    half = dense_ref.shape[0] // (block * own * 2)
    r, c = place_ref[0], place_ref[1]
    dense_ref[...] = jnp.zeros_like(dense_ref)

    @pl.loop(0, live_ref[0])
    def _(slot):
        k = row_ref[slot]
        j = col_ref[slot]
        p = (k // own) ^ c
        at_row = ((p & 1) * half + (p >> 1)) * own + k % own
        at_col = ((j // own) ^ r) * own + j % own
        dense_ref[
            pl.ds(pl.multiple_of(at_row * block, block), block),
            pl.ds(pl.multiple_of(at_col * block, block), block),
        ] = tiles_ref[slot]

    rows, columns = dense_ref.shape
    ones = jnp.ones((8, columns), BF16)
    chunk = 256

    for start in range(0, rows, chunk):
        sums = lax.dot_general(
            ones,
            dense_ref[pl.ds(start, chunk), :],
            (((1,), (1,)), ((), ())),
            preferred_element_type=F32,
        )
        for part in range(chunk // block):
            degree_ref[pl.ds(start // block + part, 1), :] = sums[
                :1, part * block : (part + 1) * block
            ]


def dense_adjacency(tiles, tile_row, tile_col, tile_live, own, rows, columns):
    place = jnp.stack([lax.axis_index("row"), lax.axis_index("col")]).astype(jnp.int32)
    block = tiles.shape[-1]
    need = rows * columns * 2 + tiles.size * 2 + rows * 16
    smem = pl.BlockSpec(memory_space=pltpu.SMEM)
    vmem = pl.BlockSpec(memory_space=pltpu.VMEM)
    return pl.pallas_call(
        functools.partial(dense_kernel, own),
        out_shape=(
            jax.ShapeDtypeStruct((rows, columns), BF16),
            jax.ShapeDtypeStruct((rows // block, block), F32),
        ),
        in_specs=[smem, smem, smem, smem, vmem],
        out_specs=(vmem, vmem),
        compiler_params=pltpu.CompilerParams(vmem_limit_bytes=need + (8 << 20)),
        cost_estimate=pl.CostEstimate(
            flops=16 * rows * columns, bytes_accessed=rows * columns * 2 + tiles.size * 2, transcendentals=0
        ),
        name="dense_adjacency",
    )(tile_row, tile_col, tile_live, place, tiles)


def gather_row(value):
    count = lax.axis_size("row")
    return jnp.concatenate([value] + [exchange(value, "row", s) for s in range(1, count)], axis=0)


def gather_col(value):
    half = lax.axis_size("col") // 2
    pieces = [value] + [exchange(value, "col", 2 * s) for s in range(1, half)]
    near = jnp.concatenate(pieces, axis=0)
    return jnp.concatenate([near, exchange(near, "col", 1)], axis=0)


def scatter_col(part, nodes):
    half = lax.axis_size("col") // 2
    middle = part.shape[0] // 2
    other = exchange(part[middle:], "col", 1)
    near = part[:middle].astype(F32) + other.astype(F32)
    sent = near.astype(BF16)
    total = near[:nodes]
    for s in range(1, half):
        total = total + exchange(sent[s * nodes : (s + 1) * nodes], "col", 2 * s).astype(F32)
    return total


def total_col(value, own):
    count = lax.axis_size("col")
    value = value + swap_halves(exchange(value, "col", 1), 1)
    mask, parts = count // 2, 2
    while mask > 1:
        value = value + swap_halves(exchange(value, "col", mask), parts)
        mask, parts = mask // 2, parts * 2
    return value


def split(value):
    high = value.astype(BF16)
    return high, (value - high.astype(F32)).astype(BF16)


def total_all(values):
    rows = lax.axis_size("row")
    size = values.shape[0] // rows
    me = lax.axis_index("row")
    blocks = values.reshape((rows, size) + values.shape[1:])
    mine = lax.dynamic_index_in_dim(blocks, me, 0, keepdims=False)
    for s in range(1, rows):
        block = lax.dynamic_index_in_dim(blocks, me ^ s, 0, keepdims=False)
        mine = mine + exchange(block.astype(BF16), "row", s).astype(F32)
    mask = 1
    while mask < lax.axis_size("col"):
        mine = mine + exchange(mine, "col", mask)
        mask *= 2
    got = jnp.stack([mine] + [exchange(mine, "row", s) for s in range(1, rows)])
    return got[jnp.arange(rows) ^ me].reshape(values.shape)


def local(
    features,
    tiles,
    tile_row,
    tile_col,
    tile_live,
    w_first,
    b_first,
    w_second,
    b_second,
    grad_logits,
):
    row_count = lax.axis_size("row")
    col_count = lax.axis_size("col")
    nodes = features.shape[0]
    block = tiles.shape[-1]
    own = nodes // block
    hidden = w_first.shape[1]
    classes = w_second.shape[1]
    rows, columns = col_count * nodes, row_count * nodes

    inputs = gather_row(features)
    cotangents = gather_col(grad_logits)
    dense, degree_part = dense_adjacency(
        tiles[0, 0], tile_row[0, 0], tile_col[0, 0], tile_live[0], own, rows, columns
    )
    first_part = jnp.dot(dense, inputs, preferred_element_type=F32).astype(BF16)
    degree = 1.0 + total_col(degree_part, own).reshape(rows)
    own_degree = degree[:nodes, None]
    first_sum = scatter_col(first_part, nodes)
    agg1 = ((first_sum + features.astype(F32)) / own_degree).astype(BF16)

    scaled = (cotangents.astype(F32) / degree[:, None]).astype(BF16)
    q_part = lax.dot_general(dense, scaled, (((0,), (0,)), ((), ())), preferred_element_type=F32)
    q_part = q_part + jnp.pad(scaled[:nodes].astype(F32), ((0, columns - nodes), (0, 0)))

    agg_all = gather_row(agg1)
    z_first = jnp.dot(agg_all, w_first, preferred_element_type=F32) + b_first
    h_float, slope = jax.vjp(lambda z: jax.nn.gelu(z, approximate=True), z_first)
    h_all = h_float.astype(BF16)
    projected = jnp.dot(h_all, w_second, preferred_element_type=F32)
    second_part = jnp.dot(dense, projected.astype(BF16), preferred_element_type=F32).astype(BF16)
    second_sum = scatter_col(second_part, nodes)
    logits = ((second_sum + projected[:nodes]) / own_degree + b_second).astype(BF16)

    q_high, q_low = split(q_part)
    rows_first = (((0,), (0,)), ((), ()))
    grad_w2 = lax.dot_general(h_all, q_high, rows_first, preferred_element_type=F32)
    grad_w2 = grad_w2 + lax.dot_general(h_all, q_low, rows_first, preferred_element_type=F32)
    d_hidden = jnp.dot(q_high, w_second.T, preferred_element_type=F32)
    d_hidden = d_hidden + jnp.dot(q_low, w_second.T, preferred_element_type=F32)
    d_first = slope(d_hidden)[0]
    grad_w1 = lax.dot_general(agg_all, d_first.astype(BF16), rows_first, preferred_element_type=F32)
    grad_b1 = jnp.sum(d_first, axis=0)
    grad_b2 = jnp.sum(grad_logits.astype(F32), axis=0)

    fin = w_first.shape[0]
    pad = ((0, 0), (0, hidden - classes))
    biases = jnp.stack([grad_b1, jnp.pad(grad_b2, pad[1:])])
    extra = -(fin + hidden + 2) % (8 * row_count * 2)
    packed = jnp.concatenate(
        [grad_w1, jnp.pad(grad_w2, pad), biases, jnp.zeros((extra, hidden), F32)], axis=0
    )
    packed = total_all(packed)
    return (
        logits,
        packed[:fin],
        packed[fin + hidden],
        packed[fin : fin + hidden, :classes],
        packed[fin + hidden + 1, :classes],
    )


def solution(mesh):
    return jax.shard_map(
        local,
        mesh=mesh,
        in_specs=(
            P(("row", "col"), None),
            P("row", "col", None, None, None),
            P("row", "col", None),
            P("row", "col", None),
            P("row", "col"),
            P(),
            P(),
            P(),
            P(),
            P(("row", "col"), None),
        ),
        out_specs=(P(("row", "col"), None), P(), P(), P(), P()),
        check_vma=False,
    )
```

```python
import functools

import jax
import jax.numpy as jnp
from jax import lax
from jax.experimental import pallas as pl
from jax.experimental.pallas import tpu as pltpu
from jax.sharding import PartitionSpec as P

BF16 = jnp.bfloat16
F32 = jnp.float32
LANES = 128
SMEM = pl.BlockSpec(memory_space=pltpu.SMEM)
VMEM = pl.BlockSpec(memory_space=pltpu.VMEM)
ANY = pl.BlockSpec(memory_space=pl.ANY)


def exchange(value, axis, mask):
    count = lax.axis_size(axis)
    return lax.ppermute(value, axis, [(i, i ^ mask) for i in range(count)])


def call(kernel, name, outs, in_specs, args, scratch=(), flops=0):
    size = sum(a.size * a.dtype.itemsize for a in args)
    size += sum(o.size * o.dtype.itemsize for o in outs)
    grant = size + (12 << 20)
    return pl.pallas_call(
        kernel,
        out_shape=tuple(outs),
        in_specs=in_specs,
        out_specs=tuple(VMEM for _ in outs),
        scratch_shapes=scratch,
        compiler_params=pltpu.CompilerParams(vmem_limit_bytes=min(grant, 60 << 20)),
        cost_estimate=pl.CostEstimate(flops=flops, bytes_accessed=size, transcendentals=0),
        name=name,
    )(*args)


def shaped(shape, dtype):
    return jax.ShapeDtypeStruct(shape, dtype)


def product(left, right, contract=((1,), (0,))):
    return lax.dot_general(left, right, (contract, ((), ())), preferred_element_type=F32)


def split(value):
    high = value.astype(BF16)
    return high, (value - high.astype(F32)).astype(BF16)


def dense_kernel(own, row_ref, col_ref, live_ref, place_ref, tiles_ref, after_ref, dense_ref, degree_ref):
    block = tiles_ref.shape[1]
    rows, columns = dense_ref.shape
    half = rows // (block * own * 2)
    r, c = place_ref[0], place_ref[1]
    dense_ref[...] = jnp.zeros_like(dense_ref)

    @pl.loop(0, live_ref[0])
    def _(slot):
        k = row_ref[slot]
        j = col_ref[slot]
        p = (k // own) ^ c
        at_row = ((p & 1) * half + (p >> 1)) * own + k % own
        at_col = ((j // own) ^ r) * own + j % own
        dense_ref[
            pl.ds(pl.multiple_of(at_row * block, block), block),
            pl.ds(pl.multiple_of(at_col * block, block), block),
        ] = tiles_ref[slot]

    ones = jnp.ones((8, columns), BF16)
    for start in range(0, rows, 2 * block):
        sums = product(ones, dense_ref[pl.ds(start, 2 * block), :], ((1,), (1,)))
        for part in range(2):
            degree_ref[pl.ds(start // block + part, 1), :] = sums[:1, part * block : (part + 1) * block]


def first_kernel(spans, dense_ref, *refs):
    pieces, (send_ref, keep_ref, held) = refs[:spans], refs[spans:]
    nodes = pieces[0].shape[0]
    for s in range(spans):
        held[pl.ds(s * nodes, nodes), :] = pieces[s][...]
    half = keep_ref.shape[0] // nodes

    @pl.loop(0, half)
    def _(s):
        at = pl.multiple_of(s * nodes, nodes)
        send_ref[pl.ds(at, nodes), :] = product(
            dense_ref[pl.ds(pl.multiple_of((half + s) * nodes, nodes), nodes), :], held[...]
        ).astype(BF16)
        keep_ref[pl.ds(at, nodes), :] = product(dense_ref[pl.ds(at, nodes), :], held[...])


def back_kernel(spans, dense_ref, near_ref, other_ref, degree_ref, *refs):
    own_ref, wide_ref = refs[:2]
    sends, turned = refs[2 : 1 + spans], refs[-1]
    classes = own_ref.shape[0]
    rows = dense_ref.shape[0]
    nodes = own_ref.shape[1]
    block = LANES
    packed = nodes + block
    half = rows // nodes // 2
    blocks = degree_ref.shape[0]
    tail = other_ref[pl.ds(half * packed, 2 * blocks), :].astype(F32)
    far = tail[:blocks] + tail[blocks:]
    far = jnp.concatenate([far[blocks // 2 :], far[: blocks // 2]], axis=0)
    degree = (1.0 + (degree_ref[...] + far)).T
    lane = lax.broadcasted_iota(jnp.int32, (block, block), 1)
    for q in range(2 * half):
        source = near_ref if q < half else other_ref
        base = (q % half) * packed
        even = jnp.broadcast_to(degree[:, 2 * q : 2 * q + 1], (block, block))
        odd = jnp.broadcast_to(degree[:, 2 * q + 1 : 2 * q + 2], (block, block))
        if q == 0:
            wide_ref[:block, :] = even
            wide_ref[block:, :] = odd
        rest = source[pl.ds(base + nodes, block), :].astype(F32)
        rolled = pltpu.roll(rest, block // 2, 1)
        low = lane < block // 2
        parts = (
            (source[pl.ds(base, block), :].astype(F32) / even, jnp.where(low, rest / even, 0.0)),
            (source[pl.ds(base + block, block), :].astype(F32) / odd, jnp.where(low, rolled / odd, 0.0)),
        )
        for b, (first, second) in enumerate(parts):
            at = pl.ds(q * nodes + b * block, block)
            turned[:block, at] = first.T.astype(BF16)
            turned[block:, at] = second.T[: classes - block].astype(BF16)
    for s in range(spans):
        part = product(turned[...], dense_ref[:, s * nodes : (s + 1) * nodes])
        if s == 0:
            own_ref[...] = part + turned[:, :nodes].astype(F32)
        else:
            sends[s - 1][...] = part.astype(BF16)


def gelu_parts(z):
    scale = 0.7978845608028654
    t = jnp.tanh(scale * (z + 0.044715 * (z * z * z)))
    value = 0.5 * z * (1.0 + t)
    slope = 0.5 * (1.0 + t) + 0.5 * z * (1.0 - t * t) * (scale * (1.0 + 3.0 * 0.044715 * (z * z)))
    return value, slope


def grad_kernel(half, spans, place_ref, near_ref, *refs):
    got, refs = refs[: half - 1], refs[half - 1 :]
    features_ref, wide_ref, own_ref, refs = refs[0], refs[1], refs[2], refs[3:]
    back, refs = refs[: spans - 1], refs[spans - 1 :]
    w1_ref, b1_ref, w2_ref, g_ref, refs = refs[0], refs[1], refs[2], refs[3], refs[4:]
    agg_ref, mine_ref, refs = refs[0], refs[1], refs[2:]
    sends, total = refs[: spans - 1], refs[-1]
    nodes = features_ref.shape[0]
    fin, hidden = w1_ref.shape
    rank = place_ref[0]
    acc = near_ref[...]
    for ref in got:
        acc = acc + ref[...].astype(F32)
    agg = ((acc + features_ref[...].astype(F32)) / wide_ref[...]).astype(BF16)
    agg_ref[...] = agg
    z = product(agg, w1_ref[...]) + b1_ref[...]
    value, slope = gelu_parts(z)
    h = value.astype(BF16)
    q = own_ref[...]
    for ref in back:
        q = q + ref[...].astype(F32)
    classes = q.shape[0]
    q = jnp.concatenate([q, jnp.zeros((2 * LANES - classes, nodes), F32)], axis=0).T
    q_high, q_low = split(q)
    w2 = w2_ref[...]
    d_first = (product(q_high, w2, ((1,), (1,))) + product(q_low, w2, ((1,), (1,)))) * slope
    turned = h.astype(F32).T.astype(BF16)
    grad_w2 = product(turned, q_high) + product(turned, q_low)
    grad_w1 = product(agg.astype(F32).T.astype(BF16), d_first.astype(BF16))
    grad_b1 = jnp.sum(d_first, axis=0, keepdims=True)
    cots = g_ref[...].astype(F32)
    left = jnp.sum(cots[:nodes], axis=0, keepdims=True)
    right = jnp.sum(cots[nodes:], axis=0, keepdims=True)
    right = right + jnp.concatenate([right[:, LANES // 2 :], right[:, : LANES // 2]], axis=1)
    a, b = fin // spans, hidden // spans
    size = total.shape[1] // 2
    total[...] = jnp.zeros_like(total)
    for t in range(spans):
        for lanes in range(2):
            at = slice(lanes * LANES, (lanes + 1) * LANES)
            total[t, lanes * size : lanes * size + a, :] = grad_w1[t * a : (t + 1) * a, at]
            total[t, lanes * size + a : lanes * size + a + b, :] = grad_w2[t * b : (t + 1) * b, at]
    total[0, a + b : a + b + 1, :] = grad_b1[:, :LANES]
    total[0, a + b + 1 : a + b + 2, :] = left
    total[0, size + a + b : size + a + b + 1, :] = grad_b1[:, LANES:]
    total[0, size + a + b + 1 : size + a + b + 2, :] = right
    mine_ref[...] = total[rank]
    for s in range(1, spans):
        sends[s - 1][:nodes, :] = agg
        sends[s - 1][nodes:, :] = total[rank ^ s].astype(BF16)


def second_kernel(spans, dense_ref, agg_ref, mine_ref, *refs):
    got, refs = refs[: spans - 1], refs[spans - 1 :]
    w1_ref, b1_ref, w2_ref, send_ref, keep_ref, even_ref, odd_ref = refs
    nodes = agg_ref.shape[0]
    block = LANES
    packed = nodes + block
    half = dense_ref.shape[0] // nodes // 2
    mine = mine_ref[...]
    for s in range(spans):
        piece = agg_ref[...] if s == 0 else got[s - 1][:nodes, :]
        if s > 0:
            mine = mine + got[s - 1][nodes:, :].astype(F32)
        value, _ = gelu_parts(product(piece, w1_ref[...]) + b1_ref[...])
        hidden = product(value.astype(BF16), w2_ref[...])
        at = pl.ds(s * nodes, nodes)
        rolled = pltpu.roll(hidden[:, block:], block // 2, 1)
        even_ref[at, :] = hidden.astype(BF16)
        odd_ref[at, :block] = hidden[:, :block].astype(BF16)
        odd_ref[at, block:] = rolled.astype(BF16)
        if s == 0:
            first = (hidden[:, :block], hidden[:block, block:] + rolled[block:])
    rounded = mine.astype(BF16)
    send_ref[half * packed :, :] = rounded
    keep_ref[half * packed :, :] = rounded.astype(F32)

    def rows_of(place):
        at = pl.multiple_of(place * nodes, nodes)
        even = product(dense_ref[pl.ds(at, block), :], even_ref[...])
        odd = product(dense_ref[pl.ds(pl.multiple_of(at + block, block), block), :], odd_ref[...])
        return even, odd

    @pl.loop(0, half)
    def _(s):
        at = pl.multiple_of(s * packed, block)
        even, odd = rows_of(half + s)
        send_ref[pl.ds(at, block), :] = even[:, :block].astype(BF16)
        send_ref[pl.ds(at + block, block), :] = odd[:, :block].astype(BF16)
        send_ref[pl.ds(at + 2 * block, block), :] = (even[:, block:] + odd[:, block:]).astype(BF16)
        even, odd = rows_of(s)
        keep_ref[pl.ds(at, block), :] = even[:, :block]
        keep_ref[pl.ds(at + block, block), :] = odd[:, :block]
        keep_ref[pl.ds(at + 2 * block, block), :] = even[:, block:] + odd[:, block:]

    keep_ref[:nodes, :] += first[0]
    keep_ref[nodes:packed, :] += first[1]


def last_kernel(spans, place_ref, *refs):
    got, (w1_ref, b1_ref, w2_ref, b2_ref) = refs[:spans], refs[spans:]
    fin, hidden = w1_ref.shape
    classes = w2_ref.shape[1]
    a, b = fin // spans, hidden // spans
    size = got[0].shape[0] // 2
    for s in range(spans):
        t = place_ref[0] ^ s
        share = got[s][...].astype(F32)
        left, right = share[:size], share[size:]
        at = pl.ds(pl.multiple_of(t * a, a), a)
        w1_ref[at, :LANES] = left[:a]
        w1_ref[at, LANES:] = right[:a]
        at = pl.ds(pl.multiple_of(t * b, b), b)
        w2_ref[at, :LANES] = left[a : a + b]
        w2_ref[at, LANES:] = right[a : a + b, : classes - LANES]

        @pl.when(t == 0)
        def _():
            b1_ref[:, :LANES] = left[a + b : a + b + 1]
            b1_ref[:, LANES:] = right[a + b : a + b + 1]
            b2_ref[:, :LANES] = left[a + b + 1 : a + b + 2]
            b2_ref[:, LANES:] = right[a + b + 1 : a + b + 2, : classes - LANES]


def pack(value):
    block = LANES
    room = ((0, 0), (0, block // 2 - (value.shape[1] - block)))
    rest = jnp.pad(value[:, block:], room)
    return jnp.concatenate(
        [value[:, :block], jnp.concatenate([rest[:block], rest[block:]], axis=1)], axis=0
    )


def tree_sum(values):
    while len(values) > 1:
        values = [a + b for a, b in zip(values[::2], values[1::2])]
    return values[0]


def swap_pairs(value, parts):
    pairs = value.reshape((parts, 2, -1) + value.shape[1:])
    return jnp.concatenate([pairs[:, 1:], pairs[:, :1]], axis=1).reshape(value.shape)


def local(
    features,
    tiles,
    tile_row,
    tile_col,
    tile_live,
    w_first,
    b_first,
    w_second,
    b_second,
    grad_logits,
):
    row_count = lax.axis_size("row")
    col_count = lax.axis_size("col")
    half = col_count // 2
    nodes, fin = features.shape
    block = tiles.shape[-1]
    own = nodes // block
    hidden = w_first.shape[1]
    classes = w_second.shape[1]
    rows, columns = col_count * nodes, row_count * nodes
    packed = nodes + block
    place = jnp.stack([lax.axis_index("row"), lax.axis_index("col")]).astype(jnp.int32)
    bias = b_first[None, :]
    w2_wide = jnp.pad(w_second, ((0, 0), (0, 2 * LANES - classes)))

    inputs = [features] + [exchange(features, "row", s) for s in range(1, row_count)]
    g_own = pack(grad_logits)
    near_g = jnp.concatenate(
        [g_own] + [exchange(g_own, "col", 2 * s) for s in range(1, half)], axis=0
    )
    dense, degree = call(
        functools.partial(dense_kernel, own),
        "dense_adjacency",
        [shaped((rows, columns), BF16), shaped((rows // block, block), F32)],
        [SMEM, SMEM, SMEM, SMEM, VMEM, ANY],
        [tile_row[0, 0], tile_col[0, 0], tile_live[0], place, tiles[0, 0], inputs[1]],
        flops=16 * rows * columns,
    )
    mask, parts = half, 2
    while mask > 1:
        degree = degree + swap_pairs(exchange(degree, "col", mask), parts)
        mask, parts = mask // 2, parts * 2
    other_g = exchange(jnp.concatenate((near_g,) + split(degree), axis=0), "col", 1)

    send, keep = call(
        functools.partial(first_kernel, row_count),
        "first_product",
        [shaped((rows // 2, fin), BF16), shaped((rows // 2, fin), F32)],
        [VMEM] * (1 + row_count),
        [dense] + inputs,
        scratch=[pltpu.VMEM((columns, fin), BF16)],
        flops=2 * rows * columns * fin,
    )
    near = keep + exchange(send, "col", 1).astype(F32)
    sent = near.astype(BF16)
    got = [exchange(sent[s * nodes : (s + 1) * nodes], "col", 2 * s) for s in range(1, half)]

    tall = -(-classes // 16) * 16
    back = call(
        functools.partial(back_kernel, row_count),
        "back_product",
        [shaped((tall, nodes), F32), shaped((nodes, LANES), F32)]
        + [shaped((tall, nodes), BF16)] * (row_count - 1),
        [VMEM] * 4,
        [dense, near_g, other_g, degree],
        scratch=[pltpu.VMEM((tall, rows), BF16)],
        flops=2 * rows * columns * tall,
    )
    q_own, wide = back[:2]
    q_got = [exchange(back[1 + s], "row", s) for s in range(1, row_count)]

    size = 2 * (fin // row_count + hidden // row_count + 16)
    out = call(
        functools.partial(grad_kernel, half, row_count),
        "gradients",
        [shaped((nodes, fin), BF16), shaped((size, LANES), F32)]
        + [shaped((nodes + size, LANES), BF16)] * (row_count - 1),
        [SMEM] + [VMEM] * (half + 3 + row_count - 1 + 4),
        [place, near[:nodes]] + got + [features, wide, q_own] + q_got + [w_first, bias, w2_wide, g_own],
        scratch=[pltpu.VMEM((row_count, size, LANES), F32)],
        flops=10 * nodes * hidden * LANES,
    )
    agg, mine = out[:2]
    rounds = [exchange(out[1 + s], "row", s) for s in range(1, row_count)]

    send, keep = call(
        functools.partial(second_kernel, row_count),
        "second_product",
        [shaped((half * packed + size, LANES), BF16), shaped((half * packed + size, LANES), F32)],
        [VMEM] * (3 + row_count - 1 + 3),
        [dense, agg, mine] + rounds + [w_first, bias, w2_wide],
        scratch=[pltpu.VMEM((columns, 2 * LANES), BF16)] * 2,
        flops=2 * rows * columns * hidden,
    )
    near = keep + exchange(send, "col", 1).astype(F32)
    sent = near.astype(BF16)
    tail = sent[half * packed :]
    got = [
        exchange(jnp.concatenate([sent[s * packed : (s + 1) * packed], tail], axis=0), "col", 2 * s)
        for s in range(1, half)
    ]
    shares = tree_sum([tail.astype(F32)] + [value[packed:].astype(F32) for value in got]).astype(BF16)
    shares = [shares] + [exchange(shares, "row", s) for s in range(1, row_count)]
    total = near[:packed]
    for value in got:
        total = total + value[:packed].astype(F32)
    rest = total[nodes:]
    cut = classes - block
    rest = jnp.concatenate([rest[:, :cut], rest[:, block // 2 : block // 2 + cut]], axis=0)
    logits = jnp.concatenate([total[:nodes], rest], axis=1)
    logits = (logits / wide[:, :1] + b_second).astype(BF16)
    grad_w1, grad_b1, grad_w2, grad_b2 = call(
        functools.partial(last_kernel, row_count),
        "place_gradients",
        [shaped((fin, hidden), F32), shaped((1, hidden), F32), shaped((hidden, classes), F32), shaped((1, classes), F32)],
        [SMEM] + [VMEM] * row_count,
        [place] + shares,
    )
    return logits, grad_w1, grad_b1[0], grad_w2, grad_b2[0]


def solution(mesh):
    return jax.shard_map(
        local,
        mesh=mesh,
        in_specs=(
            P(("row", "col"), None),
            P("row", "col", None, None, None),
            P("row", "col", None),
            P("row", "col", None),
            P("row", "col"),
            P(),
            P(),
            P(),
            P(),
            P(("row", "col"), None),
        ),
        out_specs=(P(("row", "col"), None), P(), P(), P(), P()),
        check_vma=False,
    )
```

```python
import functools

import jax
import jax.numpy as jnp
from jax import lax
from jax.experimental import pallas as pl
from jax.experimental.pallas import tpu as pltpu
from jax.sharding import PartitionSpec as P

BF16 = jnp.bfloat16
F32 = jnp.float32
LANES = 128
SMEM = pl.BlockSpec(memory_space=pltpu.SMEM)
VMEM = pl.BlockSpec(memory_space=pltpu.VMEM)
ANY = pl.BlockSpec(memory_space=pl.ANY)


def exchange(value, axis, mask):
    count = lax.axis_size(axis)
    return lax.ppermute(value, axis, [(i, i ^ mask) for i in range(count)])


def call(kernel, name, outs, in_specs, args, scratch=()):
    size = sum(a.size * a.dtype.itemsize for a in args)
    size += sum(o.size * o.dtype.itemsize for o in outs)
    grant = size + (6 << 20)
    return pl.pallas_call(
        kernel,
        out_shape=tuple(outs),
        in_specs=in_specs,
        out_specs=tuple(VMEM for _ in outs),
        scratch_shapes=scratch,
        compiler_params=pltpu.CompilerParams(vmem_limit_bytes=min(grant, 60 << 20)),
        name=name,
    )(*args)


def shaped(shape, dtype):
    return jax.ShapeDtypeStruct(shape, dtype)


def product(left, right, contract=((1,), (0,))):
    return lax.dot_general(left, right, (contract, ((), ())), preferred_element_type=F32)


def split(value):
    high = value.astype(BF16)
    return high, (value - high.astype(F32)).astype(BF16)


def dense_kernel(own, index_ref, tiles_ref, after_ref, dense_ref, degree_ref):
    slots, block, _ = tiles_ref.shape
    rows, columns = dense_ref.shape
    half = rows // (block * own * 2)
    r, c = index_ref[2 * slots + 1], index_ref[2 * slots + 2]
    dense_ref[...] = jnp.zeros_like(dense_ref)

    @pl.loop(0, index_ref[2 * slots])
    def _(slot):
        k = index_ref[slot]
        j = index_ref[slots + slot]
        p = (k // own) ^ c
        at_row = ((p & 1) * half + (p >> 1)) * own + k % own
        at_col = ((j // own) ^ r) * own + j % own
        dense_ref[
            pl.ds(pl.multiple_of(at_row * block, block), block),
            pl.ds(pl.multiple_of(at_col * block, block), block),
        ] = tiles_ref[slot]

    ones = jnp.ones((8, columns), BF16)
    for start in range(0, rows, 2 * block):
        sums = product(ones, dense_ref[pl.ds(start, 2 * block), :], ((1,), (1,)))
        for part in range(2):
            degree_ref[pl.ds(start // block + part, 1), :] = sums[:1, part * block : (part + 1) * block]


def first_kernel(spans, dense_ref, degree_ref, g_ref, far_ref, *refs):
    pieces, (send_ref, keep_ref, pair_ref, held) = refs[:spans], refs[spans:]
    pair_ref[0] = g_ref[...]
    pair_ref[1] = far_ref[...]
    nodes = pieces[0].shape[0]
    for s in range(spans):
        held[pl.ds(s * nodes, nodes), :] = pieces[s][...]
    half = keep_ref.shape[0] // nodes
    blocks = degree_ref.shape[0]
    high, low = split(degree_ref[...])
    send_ref[pl.ds(half * nodes, blocks), :] = high
    send_ref[pl.ds(half * nodes + blocks, blocks), :] = low

    @pl.loop(0, half)
    def _(s):
        at = pl.multiple_of(s * nodes, nodes)
        send_ref[pl.ds(at, nodes), :] = product(
            dense_ref[pl.ds(pl.multiple_of((half + s) * nodes, nodes), nodes), :], held[...]
        ).astype(BF16)
        keep_ref[pl.ds(at, nodes), :] = product(dense_ref[pl.ds(at, nodes), :], held[...])


def near_kernel(half, keep_ref, other_ref, part_ref, own_ref, degree_ref, *sends):
    nodes = own_ref.shape[0]
    blocks = part_ref.shape[0]
    tail = other_ref[pl.ds(half * nodes, blocks), :].astype(F32)
    tail = tail + other_ref[pl.ds(half * nodes + blocks, blocks), :].astype(F32)
    degree = part_ref[...] + jnp.concatenate([tail[blocks // 2 :], tail[: blocks // 2]], axis=0)
    degree_ref[...] = degree
    high, low = split(degree)
    own_ref[...] = keep_ref[:nodes, :] + other_ref[:nodes, :].astype(F32)
    for s in range(1, half):
        at = slice(s * nodes, (s + 1) * nodes)
        sends[s - 1][:nodes, :] = (keep_ref[at, :] + other_ref[at, :].astype(F32)).astype(BF16)
        sends[s - 1][nodes : nodes + blocks, :] = high
        sends[s - 1][nodes + blocks :, :] = low


def swapped(value, half, mask):
    own = value.shape[0] // (2 * half)
    order = [h * half + (s ^ mask) for h in range(2) for s in range(half)]
    return jnp.concatenate([value[q * own : (q + 1) * own] for q in order], axis=0)


def agg_kernel(half, near_ref, part_ref, features_ref, left_ref, right_ref, *refs):
    got, (agg_ref, degree_ref, joined_ref) = refs[: half - 1], refs[half - 1 :]
    joined_ref[: half // 2] = left_ref[...]
    joined_ref[half // 2 :] = right_ref[...]
    nodes = features_ref.shape[0]
    block = LANES
    blocks = degree_ref.shape[0]
    total = near_ref[...]
    degree = part_ref[...]
    for s, ref in enumerate(got):
        total = total + ref[:nodes, :].astype(F32)
        tail = ref[nodes : nodes + blocks, :].astype(F32) + ref[nodes + blocks :, :].astype(F32)
        degree = degree + swapped(tail, half, s + 1)
    degree = 1.0 + degree
    degree_ref[...] = degree
    upright = degree.T
    total = total + features_ref[...].astype(F32)
    for b in range(nodes // block):
        at = slice(b * block, (b + 1) * block)
        agg_ref[at, :] = (total[at] / upright[:, b : b + 1]).astype(BF16)


def tree_sum(values):
    while len(values) > 1:
        values = [a + b for a, b in zip(values[::2], values[1::2])]
    return values[0]


def gelu_parts(z):
    scale = 0.7978845608028654
    t = jnp.tanh(scale * (z + 0.044715 * (z * z * z)))
    value = 0.5 * z * (1.0 + t)
    slope = 0.5 * (1.0 + t) + 0.5 * z * (1.0 - t * t) * (scale * (1.0 + 3.0 * 0.044715 * (z * z)))
    return value, slope


def second_kernel(spans, dense_ref, after_ref, *refs):
    pieces, refs = refs[:spans], refs[spans:]
    w1_ref, b1_ref, w2_ref, send_ref, keep_ref, held = refs
    nodes = pieces[0].shape[0]
    half, tall, _ = keep_ref.shape
    classes = w2_ref.shape[0]
    for s in range(spans):
        value, _ = gelu_parts(product(pieces[s][...], w1_ref[...]) + b1_ref[...])
        hidden = product(w2_ref[...], value.astype(BF16), ((1,), (1,)))
        if tall > classes:
            hidden = jnp.concatenate([hidden, jnp.zeros((tall - classes, nodes), F32)], axis=0)
        held[:, s * nodes : (s + 1) * nodes] = hidden.astype(BF16)
        if s == 0:
            first = hidden

    @pl.loop(0, half)
    def _(s):
        at = pl.multiple_of((half + s) * nodes, nodes)
        send_ref[s] = product(held[...], dense_ref[pl.ds(at, nodes), :], ((1,), (1,))).astype(BF16)
        at = pl.multiple_of(s * nodes, nodes)
        keep_ref[s] = product(held[...], dense_ref[pl.ds(at, nodes), :], ((1,), (1,)))

    keep_ref[0] += first


def grad_kernel(spans, count, place_ref, dense_ref, degree_ref, *refs):
    pieces, refs = refs[:spans], refs[spans:]
    cots, refs = refs[:count], refs[count:]
    w1_ref, b1_ref, w2_ref, mine_ref, refs = refs[0], refs[1], refs[2], refs[3], refs[4:]
    sends, turned, total = refs[: spans - 1], refs[-2], refs[-1]
    fin, hidden = w1_ref.shape
    block = LANES
    tall = turned.shape[0]
    rank = place_ref[0]
    nodes = pieces[0].shape[0]
    classes = w2_ref.shape[0]
    for q in range(count):
        ref, at = cots[q]
        degree = jnp.concatenate([degree_ref[2 * q : 2 * q + 1, :], degree_ref[2 * q + 1 : 2 * q + 2, :]], axis=1)
        scaled = (ref[...] if at is None else ref[at]).astype(F32) / degree
        if tall > classes:
            scaled = jnp.concatenate([scaled, jnp.zeros((tall - classes, nodes), F32)], axis=0)
        turned[:, q * nodes : (q + 1) * nodes] = scaled.astype(BF16)
    w2 = jnp.concatenate([w2_ref[...].astype(F32), jnp.zeros((2 * block - classes, hidden), F32)], axis=0).astype(BF16)
    grad_w1 = jnp.zeros((fin, hidden), F32)
    grad_w2 = jnp.zeros((tall, hidden), F32)
    grad_b1 = jnp.zeros((1, hidden), F32)
    for s in range(spans):
        agg = pieces[s][...]
        value, slope = gelu_parts(product(agg, w1_ref[...]) + b1_ref[...])
        q = product(turned[...], dense_ref[:, s * nodes : (s + 1) * nodes])
        if s == 0:
            q = q + turned[:, :nodes].astype(F32)
        high, low = split(q)
        h = value.astype(BF16)
        grad_w2 = grad_w2 + product(high, h) + product(low, h)
        high, low = split(jnp.concatenate([q, jnp.zeros((2 * block - tall, nodes), F32)], axis=0).T)
        d_first = (product(high, w2) + product(low, w2)) * slope
        grad_w1 = grad_w1 + product(agg.astype(F32).T.astype(BF16), d_first.astype(BF16))
        grad_b1 = grad_b1 + jnp.sum(d_first, axis=0, keepdims=True)
    own = cots[0][0][...] if cots[0][1] is None else cots[0][0][cots[0][1]]
    grad_b2 = product(jnp.ones((8, nodes), BF16), own, ((1,), (1,)))[:1]
    a = fin // spans
    b = total.shape[1] - a - 16
    total[...] = jnp.zeros_like(total)
    for t in range(spans):
        total[t, :a, :] = grad_w1[t * a : (t + 1) * a]
        have = min(b, tall - t * b)
        if have > 0:
            total[t, a : a + have, :] = grad_w2[t * b : t * b + have]
    total[0, a + b : a + b + 1, :] = grad_b1
    total[0, a + b + 1 : a + b + 2, :classes] = grad_b2
    mine_ref[...] = total[rank]
    for s in range(1, spans):
        sends[s - 1][...] = total[rank ^ s].astype(BF16)


def core_kernel(half, keep_ref, other_ref, mine_ref, far_ref, own_ref, share_ref, *sends):
    share_ref[...] = (mine_ref[...] + far_ref[...]).astype(BF16)
    own_ref[...] = keep_ref[0] + other_ref[0].astype(F32)
    for s in range(1, half):
        sends[s - 1][...] = (keep_ref[s] + other_ref[s].astype(F32)).astype(BF16)


def last_kernel(spans, half, place_ref, total_ref, degree_ref, bias_ref, *refs):
    parts, refs = refs[: half - 1], refs[half - 1 :]
    got, (logits_ref, w1_ref, b1_ref, w2_ref, b2_ref, tall_ref) = refs[:spans], refs[spans:]
    total = total_ref[...]
    for ref in parts:
        total = total + ref[...].astype(F32)
    nodes = total.shape[1]
    classes = logits_ref.shape[0]
    degree = jnp.concatenate([degree_ref[b : b + 1, :] for b in range(nodes // LANES)], axis=1)
    bias = jnp.concatenate([bias_ref[...], jnp.zeros((1, 2 * LANES - classes), F32)], axis=1)
    bias = jnp.broadcast_to(bias, (8, 2 * LANES)).T
    logits_ref[...] = (total[:classes] / degree + bias[:classes, :1]).astype(BF16)
    fin, hidden = w1_ref.shape
    classes = w2_ref.shape[0]
    a = fin // spans
    b = got[0].shape[0] - a - 16
    for s in range(spans):
        t = place_ref[0] ^ s
        share = got[s][...].astype(F32)
        w1_ref[pl.ds(pl.multiple_of(t * a, a), a), :] = share[:a]
        tall_ref[pl.ds(pl.multiple_of(t * b, b), b), :] = share[a : a + b]

        @pl.when(t == 0)
        def _():
            b1_ref[...] = share[a + b : a + b + 1]
            b2_ref[...] = share[a + b + 1 : a + b + 2, :classes]

    w2_ref[...] = tall_ref[:classes, :]


def local(
    features,
    tiles,
    tile_row,
    tile_col,
    tile_live,
    w_first,
    b_first,
    w_second,
    b_second,
    grad_logits,
):
    row_count = lax.axis_size("row")
    col_count = lax.axis_size("col")
    half = col_count // 2
    nodes, fin = features.shape
    block = tiles.shape[-1]
    own = nodes // block
    hidden = w_first.shape[1]
    classes = w_second.shape[1]
    tall = -(-classes // 16) * 16
    rows, columns = col_count * nodes, row_count * nodes
    blocks = rows // block
    place = jnp.stack([lax.axis_index("row"), lax.axis_index("col")]).astype(jnp.int32)
    index = jnp.concatenate([tile_row[0, 0], tile_col[0, 0], tile_live[0], place])
    bias = b_first[None, :]
    w2 = w_second.T
    g_own = grad_logits.T

    inputs = [features] + [exchange(features, "row", s) for s in range(1, row_count)]
    far_g = exchange(g_own, "col", half)
    order = [0]
    mask = half
    while mask > 1:
        order = order + [s ^ (mask // 2) for s in order]
        mask //= 2

    dense, degree = call(
        functools.partial(dense_kernel, own),
        "dense_adjacency",
        [shaped((rows, columns), BF16), shaped((blocks, block), F32)],
        [SMEM, VMEM, ANY],
        [index, tiles[0, 0], inputs[1]],
    )
    send, keep, left = call(
        functools.partial(first_kernel, row_count),
        "first_product",
        [
            shaped((rows // 2 + 2 * blocks, fin), BF16),
            shaped((rows // 2, fin), F32),
            shaped((2, classes, nodes), BF16),
        ],
        [VMEM] * (4 + row_count),
        [dense, degree, g_own, far_g] + inputs,
        scratch=[pltpu.VMEM((columns, fin), BF16)],
    )
    other = exchange(send, "col", 1)
    mask = half // 2
    while mask > 2:
        left = jnp.concatenate([left, exchange(left, "col", mask)], axis=0)
        mask //= 2
    right = exchange(left, "col", mask)
    out = call(
        functools.partial(near_kernel, half),
        "first_core_sum",
        [shaped((nodes, fin), F32), shaped((blocks, block), F32)]
        + [shaped((nodes + 2 * blocks, fin), BF16)] * (half - 1),
        [VMEM] * 3,
        [keep, other, degree],
    )
    got = [exchange(out[1 + s], "col", 2 * s) for s in range(1, half)]
    agg, degree, near_g = call(
        functools.partial(agg_kernel, half),
        "first_aggregate",
        [shaped((nodes, fin), BF16), shaped((blocks, block), F32), shaped((half, classes, nodes), BF16)],
        [VMEM] * (5 + half - 1),
        [out[0], out[1], features, left, right] + got,
    )
    pieces = [agg] + [exchange(agg, "row", s) for s in range(1, row_count)]
    other_g = exchange(near_g, "col", 1)

    size = fin // row_count + -(-classes // (16 * row_count)) * 16 + 16
    out = call(
        lambda *refs: grad_kernel(
            row_count,
            col_count,
            *refs[: 3 + row_count],
            *((refs[3 + row_count + h], order.index(s)) for h in range(2) for s in range(half)),
            *refs[5 + row_count :],
        ),
        "gradients",
        [shaped((size, hidden), F32)] + [shaped((size, hidden), BF16)] * (row_count - 1),
        [SMEM] + [VMEM] * (2 + row_count + 2 + 3),
        [place, dense, degree] + pieces + [near_g, other_g, w_first, bias, w2],
        scratch=[pltpu.VMEM((tall, rows), BF16), pltpu.VMEM((row_count, size, hidden), F32)],
    )
    mine = out[0]
    for s in range(1, row_count):
        mine = mine + exchange(out[s], "row", s).astype(F32)

    send, keep = call(
        functools.partial(second_kernel, row_count),
        "second_product",
        [shaped((half, tall, nodes), BF16), shaped((half, tall, nodes), F32)],
        [VMEM, ANY] + [VMEM] * (row_count + 3),
        [dense, out[0]] + pieces + [w_first, bias, w2],
        scratch=[pltpu.VMEM((tall, columns), BF16)],
    )
    out = call(
        functools.partial(core_kernel, half),
        "second_core_sum",
        [shaped((tall, nodes), F32), shaped((size, hidden), BF16)] + [shaped((tall, nodes), BF16)] * (half - 1),
        [VMEM] * 4,
        [keep, exchange(send, "col", 1), mine, exchange(mine, "col", 1)],
    )
    shares = [out[1].astype(F32)] + [exchange(out[1], "col", 2 * s).astype(F32) for s in range(1, half)]
    share = tree_sum(shares).astype(BF16)
    parts = [exchange(out[1 + s], "col", 2 * s) for s in range(1, half)]
    shares = [share] + [exchange(share, "row", s) for s in range(1, row_count)]
    logits, grad_w1, grad_b1, grad_w2, grad_b2 = call(
        functools.partial(last_kernel, row_count, half),
        "results",
        [
            shaped((classes, nodes), BF16),
            shaped((fin, hidden), F32),
            shaped((1, hidden), F32),
            shaped((classes, hidden), F32),
            shaped((1, classes), F32),
        ],
        [SMEM] + [VMEM] * (3 + half - 1 + row_count),
        [place, out[0], degree, b_second[None, :]] + parts + shares,
        scratch=[pltpu.VMEM(((size - fin // row_count - 16) * row_count, hidden), F32)],
    )
    return logits.T, grad_w1, grad_b1[0], grad_w2.T, grad_b2[0]


def solution(mesh):
    return jax.shard_map(
        local,
        mesh=mesh,
        in_specs=(
            P(("row", "col"), None),
            P("row", "col", None, None, None),
            P("row", "col", None),
            P("row", "col", None),
            P("row", "col"),
            P(),
            P(),
            P(),
            P(),
            P(("row", "col"), None),
        ),
        out_specs=(P(("row", "col"), None), P(), P(), P(), P()),
        check_vma=False,
    )
```

```python
import functools
import math

import jax
import jax.numpy as jnp
from jax import lax
from jax.experimental import pallas as pl
from jax.experimental.pallas import tpu as pltpu
from jax.sharding import PartitionSpec as P

BF16 = jnp.bfloat16
F32 = jnp.float32
LANES = 128
GRANT = 820 << 16
VMEM = pl.BlockSpec(memory_space=pltpu.VMEM)
ANY = pl.BlockSpec(memory_space=pl.ANY)
HBM = pl.BlockSpec(memory_space=pltpu.HBM)


def exchange(value, axis, mask):
    count = lax.axis_size(axis)
    return lax.ppermute(value, axis, [(i, i ^ mask) for i in range(count)])


def call(kernel, name, outs, in_specs, args, scratch=(), grant=None):
    size = sum(math.prod(a.shape) * a.dtype.itemsize for a in [*args, *outs])
    grant = min(size + (6 << 20), 60 << 20) if grant is None else grant
    return pl.pallas_call(
        kernel,
        out_shape=tuple(outs),
        in_specs=in_specs,
        out_specs=tuple(VMEM for _ in outs),
        scratch_shapes=scratch,
        compiler_params=pltpu.CompilerParams(vmem_limit_bytes=grant),
        name=name,
    )(*args)


def shaped(shape, dtype):
    return jax.ShapeDtypeStruct(shape, dtype)


def product(left, right, contract=((1,), (0,))):
    return lax.dot_general(left, right, (contract, ((), ())), preferred_element_type=F32)


def split(value):
    high = value.astype(BF16)
    return high, (value - high.astype(F32)).astype(BF16)


def dense_kernel(own, row_hbm, col_hbm, live_hbm, tiles_hbm, features_hbm, g_hbm, next_hbm, *refs):
    dense_ref, degree_ref, held_ref, g_ref, row_ref, col_ref, live_ref, tiles_ref, done = refs
    pairs = (
        (row_hbm, row_ref),
        (col_hbm, col_ref),
        (live_hbm, live_ref),
        (tiles_hbm, tiles_ref),
        (features_hbm, held_ref.at[0]),
        (next_hbm, held_ref.at[1]),
        (g_hbm, g_ref),
    )
    copies = [pltpu.make_async_copy(a, b, done.at[n]) for n, (a, b) in enumerate(pairs)]
    for copy in copies:
        copy.start()
    block = tiles_ref.shape[-1]
    rows, columns = dense_ref.shape
    half = rows // (block * own * 2)
    r, c = lax.axis_index("row"), lax.axis_index("col")
    dense_ref[...] = jnp.zeros_like(dense_ref)
    for copy in copies[:4]:
        copy.wait()

    @pl.loop(0, live_ref[0, 0])
    def _(slot):
        k = row_ref[0, 0, slot]
        j = col_ref[0, 0, slot]
        p = (k // own) ^ c
        at_row = ((p & 1) * half + (p >> 1)) * own + k % own
        at_col = ((j // own) ^ r) * own + j % own
        dense_ref[
            pl.ds(pl.multiple_of(at_row * block, block), block),
            pl.ds(pl.multiple_of(at_col * block, block), block),
        ] = tiles_ref[0, 0, slot]

    ones = jnp.ones((8, columns), BF16)
    for start in range(0, rows, 2 * block):
        sums = product(ones, dense_ref[pl.ds(start, 2 * block), :], ((1,), (1,)))
        for part in range(2):
            degree_ref[pl.ds(start // block + part, 1), :] = sums[:1, part * block : (part + 1) * block]
    for copy in copies[4:]:
        copy.wait()


def first_kernel(spans, dense_ref, degree_ref, g_ref, far_ref, pair_in_ref, *refs):
    pieces, (send_ref, keep_ref, pair_ref, held) = refs[: spans - 2], refs[spans - 2 :]
    pair_ref[0] = g_ref[...]
    pair_ref[1] = far_ref[...]
    nodes = g_ref.shape[1]
    held[pl.ds(0, nodes), :] = pair_in_ref[0]
    held[pl.ds(nodes, nodes), :] = pair_in_ref[1]
    for s in range(2, spans):
        held[pl.ds(s * nodes, nodes), :] = pieces[s - 2][...]
    half = keep_ref.shape[0] // nodes
    blocks = degree_ref.shape[0]
    high, low = split(degree_ref[...])
    send_ref[pl.ds(half * nodes, blocks), :] = high
    send_ref[pl.ds(half * nodes + blocks, blocks), :] = low

    @pl.loop(0, half)
    def _(s):
        at = pl.multiple_of(s * nodes, nodes)
        send_ref[pl.ds(at, nodes), :] = product(
            dense_ref[pl.ds(pl.multiple_of((half + s) * nodes, nodes), nodes), :], held[...]
        ).astype(BF16)
        keep_ref[pl.ds(at, nodes), :] = product(dense_ref[pl.ds(at, nodes), :], held[...])


def near_kernel(half, keep_ref, other_ref, part_ref, own_ref, degree_ref, *sends):
    nodes = own_ref.shape[0]
    blocks = part_ref.shape[0]
    tail = other_ref[pl.ds(half * nodes, blocks), :].astype(F32)
    tail = tail + other_ref[pl.ds(half * nodes + blocks, blocks), :].astype(F32)
    degree = part_ref[...] + jnp.concatenate([tail[blocks // 2 :], tail[: blocks // 2]], axis=0)
    degree_ref[...] = degree
    high, low = split(degree)
    own_ref[...] = keep_ref[:nodes, :] + other_ref[:nodes, :].astype(F32)
    for s in range(1, half):
        at = slice(s * nodes, (s + 1) * nodes)
        sends[s - 1][:nodes, :] = (keep_ref[at, :] + other_ref[at, :].astype(F32)).astype(BF16)
        sends[s - 1][nodes : nodes + blocks, :] = high
        sends[s - 1][nodes + blocks :, :] = low


def swapped(value, half, mask):
    own = value.shape[0] // (2 * half)
    order = [h * half + (s ^ mask) for h in range(2) for s in range(half)]
    return jnp.concatenate([value[q * own : (q + 1) * own] for q in order], axis=0)


def agg_kernel(half, near_ref, part_ref, held_ref, left_ref, right_ref, *refs):
    got, (agg_ref, degree_ref, joined_ref) = refs[: half - 1], refs[half - 1 :]
    joined_ref[: half // 2] = left_ref[...]
    joined_ref[half // 2 :] = right_ref[...]
    nodes = held_ref.shape[1]
    block = LANES
    blocks = degree_ref.shape[0]
    total = near_ref[...]
    degree = part_ref[...]
    for s, ref in enumerate(got):
        total = total + ref[:nodes, :].astype(F32)
        tail = ref[nodes : nodes + blocks, :].astype(F32) + ref[nodes + blocks :, :].astype(F32)
        degree = degree + swapped(tail, half, s + 1)
    degree = 1.0 + degree
    degree_ref[...] = degree
    upright = degree.T
    total = total + held_ref[0].astype(F32)
    for b in range(nodes // block):
        at = slice(b * block, (b + 1) * block)
        agg_ref[at, :] = (total[at] / upright[:, b : b + 1]).astype(BF16)


def tree_sum(values):
    while len(values) > 1:
        values = [a + b for a, b in zip(values[::2], values[1::2])]
    return values[0]


def gelu_parts(z):
    scale = 0.7978845608028654
    t = jnp.tanh(scale * (z + 0.044715 * (z * z * z)))
    value = 0.5 * z * (1.0 + t)
    slope = 0.5 * (1.0 + t) + 0.5 * z * (1.0 - t * t) * (scale * (1.0 + 3.0 * 0.044715 * (z * z)))
    return value, slope


def second_kernel(dense_ref, hidden_ref, first_ref, after_ref, send_ref, keep_ref):
    half, _, nodes = keep_ref.shape

    @pl.loop(0, half)
    def _(s):
        at = pl.multiple_of((half + s) * nodes, nodes)
        send_ref[s] = product(hidden_ref[...], dense_ref[pl.ds(at, nodes), :], ((1,), (1,))).astype(BF16)
        at = pl.multiple_of(s * nodes, nodes)
        keep_ref[s] = product(hidden_ref[...], dense_ref[pl.ds(at, nodes), :], ((1,), (1,)))

    keep_ref[0] += first_ref[...]


def back_kernel(spans, order, dense_ref, degree_ref, near_ref, other_ref, back_ref, turned):
    _, classes, nodes = near_ref.shape
    tall = turned.shape[0]
    for q in range(2 * len(order)):
        source = near_ref if q < len(order) else other_ref
        degree = jnp.concatenate([degree_ref[2 * q : 2 * q + 1, :], degree_ref[2 * q + 1 : 2 * q + 2, :]], axis=1)
        scaled = source[order.index(q % len(order))].astype(F32) / degree
        if tall > classes:
            scaled = jnp.concatenate([scaled, jnp.zeros((tall - classes, nodes), F32)], axis=0)
        turned[:, q * nodes : (q + 1) * nodes] = scaled.astype(BF16)
    for s in range(spans):
        part = product(turned[...], dense_ref[:, s * nodes : (s + 1) * nodes])
        if s == 0:
            part = part + turned[:, :nodes].astype(F32)
        back_ref[s] = part


def grad_kernel(spans, back_ref, g_ref, *refs):
    pieces, refs = refs[:spans], refs[spans:]
    w1_ref, b1_ref, w2_ref, mine_ref, hidden_ref, first_ref, refs = refs[0], refs[1], refs[2], refs[3], refs[4], refs[5], refs[6:]
    sends, total = refs[: spans - 1], refs[-1]
    fin, hidden = w1_ref.shape
    block = LANES
    tall = back_ref.shape[1]
    rank = lax.axis_index("row")
    nodes = pieces[0].shape[0]
    classes = w2_ref.shape[0]
    w2 = jnp.concatenate([w2_ref[...].astype(F32), jnp.zeros((2 * block - classes, hidden), F32)], axis=0).astype(BF16)
    grad_w1 = jnp.zeros((fin, hidden), F32)
    grad_w2 = jnp.zeros((tall, hidden), F32)
    grad_b1 = jnp.zeros((1, hidden), F32)
    for s in range(spans):
        agg = pieces[s][...]
        value, slope = gelu_parts(product(agg, w1_ref[...]) + b1_ref[...])
        h = value.astype(BF16)
        projected = product(w2, h, ((1,), (1,)))[:tall]
        hidden_ref[:, s * nodes : (s + 1) * nodes] = projected.astype(BF16)
        if s == 0:
            first_ref[...] = projected
        q = back_ref[s]
        high, low = split(q)
        grad_w2 = grad_w2 + product(high, h) + product(low, h)
        high, low = split(jnp.concatenate([q, jnp.zeros((2 * block - tall, nodes), F32)], axis=0).T)
        d_first = (product(high, w2) + product(low, w2)) * slope
        grad_w1 = grad_w1 + product(agg.astype(F32).T.astype(BF16), d_first.astype(BF16))
        grad_b1 = grad_b1 + jnp.sum(d_first, axis=0, keepdims=True)
    grad_b2 = product(jnp.ones((8, nodes), BF16), g_ref[...], ((1,), (1,)))[:1]
    a = fin // spans
    b = total.shape[1] - a - 16
    total[...] = jnp.zeros_like(total)
    for t in range(spans):
        total[t, :a, :] = grad_w1[t * a : (t + 1) * a]
        have = min(b, tall - t * b)
        if have > 0:
            total[t, a : a + have, :] = grad_w2[t * b : t * b + have]
    total[0, a + b : a + b + 1, :] = grad_b1
    total[0, a + b + 1 : a + b + 2, :classes] = grad_b2
    mine_ref[...] = total[rank]
    for s in range(1, spans):
        sends[s - 1][...] = total[rank ^ s].astype(BF16)


def core_kernel(half, keep_ref, other_ref, mine_ref, far_ref, own_ref, share_ref, *sends):
    share_ref[...] = (mine_ref[...] + far_ref[...]).astype(BF16)
    own_ref[...] = keep_ref[0] + other_ref[0].astype(F32)
    for s in range(1, half):
        sends[s - 1][...] = (keep_ref[s] + other_ref[s].astype(F32)).astype(BF16)


def last_kernel(spans, half, total_ref, degree_ref, bias_ref, *refs):
    parts, refs = refs[: half - 1], refs[half - 1 :]
    got, (logits_ref, w1_ref, b1_ref, w2_ref, b2_ref, tall_ref) = refs[:spans], refs[spans:]
    total = total_ref[...]
    for ref in parts:
        total = total + ref[...].astype(F32)
    nodes = total.shape[1]
    classes = logits_ref.shape[0]
    degree = jnp.concatenate([degree_ref[b : b + 1, :] for b in range(nodes // LANES)], axis=1)
    bias = jnp.concatenate([bias_ref[...], jnp.zeros((1, 2 * LANES - classes), F32)], axis=1)
    bias = jnp.broadcast_to(bias, (8, 2 * LANES)).T
    logits_ref[...] = (total[:classes] / degree + bias[:classes, :1]).astype(BF16)
    fin, hidden = w1_ref.shape
    classes = w2_ref.shape[0]
    a = fin // spans
    b = got[0].shape[0] - a - 16
    for s in range(spans):
        t = lax.axis_index("row") ^ s
        share = got[s][...].astype(F32)
        w1_ref[pl.ds(pl.multiple_of(t * a, a), a), :] = share[:a]
        tall_ref[pl.ds(pl.multiple_of(t * b, b), b), :] = share[a : a + b]

        @pl.when(t == 0)
        def _():
            b1_ref[...] = share[a + b : a + b + 1]
            b2_ref[...] = share[a + b + 1 : a + b + 2, :classes]

    w2_ref[...] = tall_ref[:classes, :]


def local(
    features,
    tiles,
    tile_row,
    tile_col,
    tile_live,
    w_first,
    b_first,
    w_second,
    b_second,
    grad_logits,
):
    row_count = lax.axis_size("row")
    col_count = lax.axis_size("col")
    half = col_count // 2
    nodes, fin = features.shape
    block = tiles.shape[-1]
    own = nodes // block
    hidden = w_first.shape[1]
    classes = w_second.shape[1]
    tall = -(-classes // 16) * 16
    rows, columns = col_count * nodes, row_count * nodes
    blocks = rows // block
    bias = b_first[None, :]
    w2 = w_second.T
    g_own = grad_logits.T

    inputs = [features] + [exchange(features, "row", s) for s in range(1, row_count)]
    far_g = exchange(g_own, "col", half)
    order = [0]
    mask = half
    while mask > 1:
        order = order + [s ^ (mask // 2) for s in order]
        mask //= 2

    whole = rows * columns * 2 <= 4 << 20
    keep_in = pltpu.VMEM if whole else shaped
    dense, degree, held, own_g = call(
        functools.partial(dense_kernel, own),
        "dense_adjacency",
        [
            keep_in((rows, columns), BF16),
            keep_in((blocks, block), F32),
            keep_in((2, nodes, fin), BF16),
            keep_in(g_own.shape, BF16),
        ],
        [HBM] * 7,
        [tile_row, tile_col, tile_live, tiles, features, g_own, inputs[1]],
        scratch=[
            pltpu.SMEM(tile_row.shape, jnp.int32),
            pltpu.SMEM(tile_col.shape, jnp.int32),
            pltpu.SMEM(tile_live.shape, jnp.int32),
            pltpu.VMEM(tiles.shape, BF16),
            pltpu.SemaphoreType.DMA((7,)),
        ],
        grant=GRANT if whole else 60 << 20,
    )
    send, keep, left = call(
        functools.partial(first_kernel, row_count),
        "first_product",
        [
            shaped((rows // 2 + 2 * blocks, fin), BF16),
            shaped((rows // 2, fin), F32),
            shaped((2, classes, nodes), BF16),
        ],
        [VMEM] * (5 + row_count - 2),
        [dense, degree, own_g, far_g, held] + inputs[2:],
        scratch=[pltpu.VMEM((columns, fin), BF16)],
    )
    other = exchange(send, "col", 1)
    mask = half // 2
    while mask > 2:
        left = jnp.concatenate([left, exchange(left, "col", mask)], axis=0)
        mask //= 2
    right = exchange(left, "col", mask)
    out = call(
        functools.partial(near_kernel, half),
        "first_core_sum",
        [shaped((nodes, fin), F32), shaped((blocks, block), F32)]
        + [shaped((nodes + 2 * blocks, fin), BF16)] * (half - 1),
        [VMEM] * 3,
        [keep, other, degree],
    )
    got = [exchange(out[1 + s], "col", 2 * s) for s in range(1, half)]
    agg, degree, near_g = call(
        functools.partial(agg_kernel, half),
        "first_aggregate",
        [shaped((nodes, fin), BF16), shaped((blocks, block), F32), shaped((half, classes, nodes), BF16)],
        [VMEM] * (5 + half - 1),
        [out[0], out[1], held, left, right] + got,
    )
    pieces = [agg] + [exchange(agg, "row", s) for s in range(1, row_count)]
    other_g = exchange(near_g, "col", 1)

    size = fin // row_count + -(-classes // (16 * row_count)) * 16 + 16
    back = call(
        functools.partial(back_kernel, row_count, order),
        "back_product",
        [shaped((row_count, tall, nodes), F32)],
        [VMEM] * 4,
        [dense, degree, near_g, other_g],
        scratch=[pltpu.VMEM((tall, rows), BF16)],
    )[0]
    out = call(
        functools.partial(grad_kernel, row_count),
        "gradients",
        [shaped((size, hidden), F32), shaped((tall, columns), BF16), shaped((tall, nodes), F32)]
        + [shaped((size, hidden), BF16)] * (row_count - 1),
        [VMEM] * (2 + row_count + 3),
        [back, own_g] + pieces + [w_first, bias, w2],
        scratch=[pltpu.VMEM((row_count, size, hidden), F32)],
    )
    mine = out[0]
    for s in range(1, row_count):
        mine = mine + exchange(out[2 + s], "row", s).astype(F32)

    send, keep = call(
        second_kernel,
        "second_product",
        [shaped((half, tall, nodes), BF16), shaped((half, tall, nodes), F32)],
        [VMEM, VMEM, VMEM, ANY],
        [dense, out[1], out[2], out[0]],
    )
    out = call(
        functools.partial(core_kernel, half),
        "second_core_sum",
        [shaped((tall, nodes), F32), shaped((size, hidden), BF16)] + [shaped((tall, nodes), BF16)] * (half - 1),
        [VMEM] * 4,
        [keep, exchange(send, "col", 1), mine, exchange(mine, "col", 1)],
    )
    shares = [out[1].astype(F32)] + [exchange(out[1], "col", 2 * s).astype(F32) for s in range(1, half)]
    share = tree_sum(shares).astype(BF16)
    parts = [exchange(out[1 + s], "col", 2 * s) for s in range(1, half)]
    shares = [share] + [exchange(share, "row", s) for s in range(1, row_count)]
    logits, grad_w1, grad_b1, grad_w2, grad_b2 = call(
        functools.partial(last_kernel, row_count, half),
        "results",
        [
            shaped((classes, nodes), BF16),
            shaped((fin, hidden), F32),
            shaped((1, hidden), F32),
            shaped((classes, hidden), F32),
            shaped((1, classes), F32),
        ],
        [VMEM] * (3 + half - 1 + row_count),
        [out[0], degree, b_second[None, :]] + parts + shares,
        scratch=[pltpu.VMEM(((size - fin // row_count - 16) * row_count, hidden), F32)],
    )
    return logits.T, grad_w1, grad_b1[0], grad_w2.T, grad_b2[0]


def solution(mesh):
    return jax.shard_map(
        local,
        mesh=mesh,
        in_specs=(
            P(("row", "col"), None),
            P("row", "col", None, None, None),
            P("row", "col", None),
            P("row", "col", None),
            P("row", "col"),
            P(),
            P(),
            P(),
            P(),
            P(("row", "col"), None),
        ),
        out_specs=(P(("row", "col"), None), P(), P(), P(), P()),
        check_vma=False,
    )
```

```python
import functools
import math

import jax
import jax.numpy as jnp
from jax import lax
from jax.experimental import pallas as pl
from jax.experimental.pallas import tpu as pltpu
from jax.sharding import PartitionSpec as P

BF16 = jnp.bfloat16
F32 = jnp.float32
LANES = 128
GRANT = 820 << 16
VMEM = pl.BlockSpec(memory_space=pltpu.VMEM)
ANY = pl.BlockSpec(memory_space=pl.ANY)
HBM = pl.BlockSpec(memory_space=pltpu.HBM)


def exchange(value, axis, mask):
    count = lax.axis_size(axis)
    return lax.ppermute(value, axis, [(i, i ^ mask) for i in range(count)])


def call(kernel, name, outs, in_specs, args, scratch=(), grant=None):
    size = sum(math.prod(a.shape) * a.dtype.itemsize for a in [*args, *outs])
    grant = min(size + (6 << 20), 60 << 20) if grant is None else grant
    return pl.pallas_call(
        kernel,
        out_shape=tuple(outs),
        in_specs=in_specs,
        out_specs=tuple(VMEM for _ in outs),
        scratch_shapes=scratch,
        compiler_params=pltpu.CompilerParams(vmem_limit_bytes=grant),
        name=name,
    )(*args)


def shaped(shape, dtype):
    return jax.ShapeDtypeStruct(shape, dtype)


def product(left, right, contract=((1,), (0,))):
    return lax.dot_general(left, right, (contract, ((), ())), preferred_element_type=F32)


def split(value):
    high = value.astype(BF16)
    return high, (value - high.astype(F32)).astype(BF16)


def dense_kernel(own, row_hbm, col_hbm, live_hbm, tiles_hbm, features_hbm, g_hbm, next_hbm, *refs):
    dense_ref, held_ref, g_ref, row_ref, col_ref, live_ref, tiles_ref, done = refs
    pairs = (
        (row_hbm, row_ref),
        (col_hbm, col_ref),
        (live_hbm, live_ref),
        (tiles_hbm, tiles_ref),
        (features_hbm, held_ref.at[0]),
        (next_hbm, held_ref.at[1]),
        (g_hbm, g_ref),
    )
    copies = [pltpu.make_async_copy(a, b, done.at[n]) for n, (a, b) in enumerate(pairs)]
    for copy in copies:
        copy.start()
    block = tiles_ref.shape[-1]
    rows, columns = dense_ref.shape
    half = rows // (block * own * 2)
    r, c = lax.axis_index("row"), lax.axis_index("col")
    dense_ref[...] = jnp.zeros_like(dense_ref)
    for copy in copies[:4]:
        copy.wait()

    @pl.loop(0, live_ref[0, 0])
    def _(slot):
        k = row_ref[0, 0, slot]
        j = col_ref[0, 0, slot]
        p = (k // own) ^ c
        at_row = ((p & 1) * half + (p >> 1)) * own + k % own
        at_col = ((j // own) ^ r) * own + j % own
        dense_ref[
            pl.ds(pl.multiple_of(at_row * block, block), block),
            pl.ds(pl.multiple_of(at_col * block, block), block),
        ] = tiles_ref[0, 0, slot]

    for copy in copies[4:]:
        copy.wait()


def first_kernel(spans, dense_ref, g_ref, far_ref, pair_in_ref, *refs):
    pieces, (send_ref, keep_ref, degree_ref, pair_ref, held) = refs[: spans - 2], refs[spans - 2 :]
    pair_ref[0] = g_ref[...]
    pair_ref[1] = far_ref[...]
    nodes = g_ref.shape[1]
    fin = pair_in_ref.shape[2]
    block = LANES
    for s in range(spans):
        held[pl.ds(s * nodes, nodes), :fin] = pair_in_ref[s] if s < 2 else pieces[s - 2][...]
    held[:, fin:] = jnp.ones((held.shape[0], block), BF16)
    half = keep_ref.shape[0] // nodes
    blocks = degree_ref.shape[0]
    line = lax.broadcasted_iota(jnp.int32, (block, block), 0) == lax.broadcasted_iota(jnp.int32, (block, block), 1)

    for s in range(2 * half):
        out = product(dense_ref[pl.ds(s * nodes, nodes), :], held[...])
        if s < half:
            keep_ref[pl.ds(s * nodes, nodes), :] = out[:, :fin]
        else:
            send_ref[pl.ds((s - half) * nodes, nodes), :] = out[:, :fin].astype(BF16)
        for b in range(nodes // block):
            sums = jnp.where(line, out[b * block : (b + 1) * block, fin:], 0.0)
            at = s * (nodes // block) + b
            degree_ref[at : at + 1, :] = jnp.sum(sums, axis=0, keepdims=True)
    high, low = split(degree_ref[...])
    send_ref[pl.ds(half * nodes, blocks), :] = high
    send_ref[pl.ds(half * nodes + blocks, blocks), :] = low


def near_kernel(half, keep_ref, other_ref, part_ref, own_ref, degree_ref, *sends):
    nodes = own_ref.shape[0]
    blocks = part_ref.shape[0]
    tail = other_ref[pl.ds(half * nodes, blocks), :].astype(F32)
    tail = tail + other_ref[pl.ds(half * nodes + blocks, blocks), :].astype(F32)
    degree = part_ref[...] + jnp.concatenate([tail[blocks // 2 :], tail[: blocks // 2]], axis=0)
    degree_ref[...] = degree
    high, low = split(degree)
    own_ref[...] = keep_ref[:nodes, :] + other_ref[:nodes, :].astype(F32)
    for s in range(1, half):
        at = slice(s * nodes, (s + 1) * nodes)
        sends[s - 1][:nodes, :] = (keep_ref[at, :] + other_ref[at, :].astype(F32)).astype(BF16)
        sends[s - 1][nodes : nodes + blocks, :] = high
        sends[s - 1][nodes + blocks :, :] = low


def swapped(value, half, mask):
    own = value.shape[0] // (2 * half)
    order = [h * half + (s ^ mask) for h in range(2) for s in range(half)]
    return jnp.concatenate([value[q * own : (q + 1) * own] for q in order], axis=0)


def agg_kernel(half, near_ref, part_ref, held_ref, left_ref, right_ref, *refs):
    got, (agg_ref, degree_ref, joined_ref) = refs[: half - 1], refs[half - 1 :]
    joined_ref[: half // 2] = left_ref[...]
    joined_ref[half // 2 :] = right_ref[...]
    nodes = held_ref.shape[1]
    block = LANES
    blocks = degree_ref.shape[0]
    total = near_ref[...]
    degree = part_ref[...]
    for s, ref in enumerate(got):
        total = total + ref[:nodes, :].astype(F32)
        tail = ref[nodes : nodes + blocks, :].astype(F32) + ref[nodes + blocks :, :].astype(F32)
        degree = degree + swapped(tail, half, s + 1)
    degree = 1.0 + degree
    degree_ref[...] = degree
    upright = degree.T
    total = total + held_ref[0].astype(F32)
    for b in range(nodes // block):
        at = slice(b * block, (b + 1) * block)
        agg_ref[at, :] = (total[at] / upright[:, b : b + 1]).astype(BF16)


def tree_sum(values):
    while len(values) > 1:
        values = [a + b for a, b in zip(values[::2], values[1::2])]
    return values[0]


def gelu_parts(z):
    scale = 0.7978845608028654
    t = jnp.tanh(scale * (z + 0.044715 * (z * z * z)))
    value = 0.5 * z * (1.0 + t)
    slope = 0.5 * (1.0 + t) + 0.5 * z * (1.0 - t * t) * (scale * (1.0 + 3.0 * 0.044715 * (z * z)))
    return value, slope


def second_kernel(dense_ref, hidden_ref, first_ref, after_ref, send_ref, keep_ref):
    half, _, nodes = keep_ref.shape

    @pl.loop(0, half)
    def _(s):
        at = pl.multiple_of((half + s) * nodes, nodes)
        send_ref[s] = product(hidden_ref[...], dense_ref[pl.ds(at, nodes), :], ((1,), (1,))).astype(BF16)
        at = pl.multiple_of(s * nodes, nodes)
        keep_ref[s] = product(hidden_ref[...], dense_ref[pl.ds(at, nodes), :], ((1,), (1,)))

    keep_ref[0] += first_ref[...]


def back_kernel(spans, order, dense_ref, degree_ref, near_ref, other_ref, back_ref, turned):
    _, classes, nodes = near_ref.shape
    tall = turned.shape[0]
    for q in range(2 * len(order)):
        source = near_ref if q < len(order) else other_ref
        degree = jnp.concatenate([degree_ref[2 * q : 2 * q + 1, :], degree_ref[2 * q + 1 : 2 * q + 2, :]], axis=1)
        scaled = source[order.index(q % len(order))].astype(F32) / degree
        if tall > classes:
            scaled = jnp.concatenate([scaled, jnp.zeros((tall - classes, nodes), F32)], axis=0)
        turned[:, q * nodes : (q + 1) * nodes] = scaled.astype(BF16)
    for s in range(spans):
        part = product(turned[...], dense_ref[:, s * nodes : (s + 1) * nodes])
        if s == 0:
            part = part + turned[:, :nodes].astype(F32)
        back_ref[s] = part


def grad_kernel(spans, back_ref, g_ref, *refs):
    pieces, refs = refs[:spans], refs[spans:]
    w1_ref, b1_ref, w2_ref, mine_ref, hidden_ref, first_ref, refs = refs[0], refs[1], refs[2], refs[3], refs[4], refs[5], refs[6:]
    sends, total = refs[: spans - 1], refs[-1]
    fin, hidden = w1_ref.shape
    block = LANES
    tall = back_ref.shape[1]
    rank = lax.axis_index("row")
    nodes = pieces[0].shape[0]
    classes = w2_ref.shape[0]
    w2 = jnp.concatenate([w2_ref[...].astype(F32), jnp.zeros((2 * block - classes, hidden), F32)], axis=0).astype(BF16)
    grad_w1 = jnp.zeros((fin, hidden), F32)
    grad_w2 = jnp.zeros((tall, hidden), F32)
    grad_b1 = jnp.zeros((1, hidden), F32)
    for s in range(spans):
        agg = pieces[s][...]
        value, slope = gelu_parts(product(agg, w1_ref[...]) + b1_ref[...])
        h = value.astype(BF16)
        projected = product(w2, h, ((1,), (1,)))[:tall]
        hidden_ref[:, s * nodes : (s + 1) * nodes] = projected.astype(BF16)
        if s == 0:
            first_ref[...] = projected
        q = back_ref[s]
        high, low = split(q)
        grad_w2 = grad_w2 + product(high, h) + product(low, h)
        high, low = split(jnp.concatenate([q, jnp.zeros((2 * block - tall, nodes), F32)], axis=0).T)
        d_first = (product(high, w2) + product(low, w2)) * slope
        grad_w1 = grad_w1 + product(agg.astype(F32).T.astype(BF16), d_first.astype(BF16))
        grad_b1 = grad_b1 + jnp.sum(d_first, axis=0, keepdims=True)
    grad_b2 = product(jnp.ones((8, nodes), BF16), g_ref[...], ((1,), (1,)))[:1]
    a = fin // spans
    b = total.shape[1] - a - 16
    total[...] = jnp.zeros_like(total)
    for t in range(spans):
        total[t, :a, :] = grad_w1[t * a : (t + 1) * a]
        have = min(b, tall - t * b)
        if have > 0:
            total[t, a : a + have, :] = grad_w2[t * b : t * b + have]
    total[0, a + b : a + b + 1, :] = grad_b1
    total[0, a + b + 1 : a + b + 2, :classes] = grad_b2
    mine_ref[...] = total[rank]
    for s in range(1, spans):
        sends[s - 1][...] = total[rank ^ s].astype(BF16)


def core_kernel(half, keep_ref, other_ref, mine_ref, far_ref, own_ref, share_ref, *sends):
    share_ref[...] = (mine_ref[...] + far_ref[...]).astype(BF16)
    own_ref[...] = keep_ref[0] + other_ref[0].astype(F32)
    for s in range(1, half):
        sends[s - 1][...] = (keep_ref[s] + other_ref[s].astype(F32)).astype(BF16)


def last_kernel(spans, half, total_ref, degree_ref, bias_ref, *refs):
    parts, refs = refs[: half - 1], refs[half - 1 :]
    got, (logits_ref, w1_ref, b1_ref, w2_ref, b2_ref, tall_ref) = refs[:spans], refs[spans:]
    total = total_ref[...]
    for ref in parts:
        total = total + ref[...].astype(F32)
    nodes = total.shape[1]
    classes = logits_ref.shape[0]
    degree = jnp.concatenate([degree_ref[b : b + 1, :] for b in range(nodes // LANES)], axis=1)
    bias = jnp.concatenate([bias_ref[...], jnp.zeros((1, 2 * LANES - classes), F32)], axis=1)
    bias = jnp.broadcast_to(bias, (8, 2 * LANES)).T
    logits_ref[...] = (total[:classes] / degree + bias[:classes, :1]).astype(BF16)
    fin, hidden = w1_ref.shape
    classes = w2_ref.shape[0]
    a = fin // spans
    b = got[0].shape[0] - a - 16
    for s in range(spans):
        t = lax.axis_index("row") ^ s
        share = got[s][...].astype(F32)
        w1_ref[pl.ds(pl.multiple_of(t * a, a), a), :] = share[:a]
        tall_ref[pl.ds(pl.multiple_of(t * b, b), b), :] = share[a : a + b]

        @pl.when(t == 0)
        def _():
            b1_ref[...] = share[a + b : a + b + 1]
            b2_ref[...] = share[a + b + 1 : a + b + 2, :classes]

    w2_ref[...] = tall_ref[:classes, :]


def local(
    features,
    tiles,
    tile_row,
    tile_col,
    tile_live,
    w_first,
    b_first,
    w_second,
    b_second,
    grad_logits,
):
    row_count = lax.axis_size("row")
    col_count = lax.axis_size("col")
    half = col_count // 2
    nodes, fin = features.shape
    block = tiles.shape[-1]
    own = nodes // block
    hidden = w_first.shape[1]
    classes = w_second.shape[1]
    tall = -(-classes // 16) * 16
    rows, columns = col_count * nodes, row_count * nodes
    blocks = rows // block
    bias = b_first[None, :]
    w2 = w_second.T
    g_own = grad_logits.T

    inputs = [features] + [exchange(features, "row", s) for s in range(1, row_count)]
    far_g = exchange(g_own, "col", half)
    order = [0]
    mask = half
    while mask > 1:
        order = order + [s ^ (mask // 2) for s in order]
        mask //= 2

    whole = rows * columns * 2 <= 4 << 20
    keep_in = pltpu.VMEM if whole else shaped
    dense, held, own_g = call(
        functools.partial(dense_kernel, own),
        "dense_adjacency",
        [
            keep_in((rows, columns), BF16),
            keep_in((2, nodes, fin), BF16),
            keep_in(g_own.shape, BF16),
        ],
        [HBM] * 7,
        [tile_row, tile_col, tile_live, tiles, features, g_own, inputs[1]],
        scratch=[
            pltpu.SMEM(tile_row.shape, jnp.int32),
            pltpu.SMEM(tile_col.shape, jnp.int32),
            pltpu.SMEM(tile_live.shape, jnp.int32),
            pltpu.VMEM(tiles.shape, BF16),
            pltpu.SemaphoreType.DMA((7,)),
        ],
        grant=GRANT if whole else 60 << 20,
    )
    send, keep, degree, left = call(
        functools.partial(first_kernel, row_count),
        "first_product",
        [
            shaped((rows // 2 + 2 * blocks, fin), BF16),
            shaped((rows // 2, fin), F32),
            shaped((blocks, block), F32),
            shaped((2, classes, nodes), BF16),
        ],
        [VMEM] * (2 + row_count),
        [dense, own_g, far_g, held] + inputs[2:],
        scratch=[pltpu.VMEM((columns, fin + LANES), BF16)],
    )
    other = exchange(send, "col", 1)
    mask = half // 2
    while mask > 2:
        left = jnp.concatenate([left, exchange(left, "col", mask)], axis=0)
        mask //= 2
    right = exchange(left, "col", mask)
    out = call(
        functools.partial(near_kernel, half),
        "first_core_sum",
        [shaped((nodes, fin), F32), shaped((blocks, block), F32)]
        + [shaped((nodes + 2 * blocks, fin), BF16)] * (half - 1),
        [VMEM] * 3,
        [keep, other, degree],
    )
    got = [exchange(out[1 + s], "col", 2 * s) for s in range(1, half)]
    agg, degree, near_g = call(
        functools.partial(agg_kernel, half),
        "first_aggregate",
        [shaped((nodes, fin), BF16), shaped((blocks, block), F32), shaped((half, classes, nodes), BF16)],
        [VMEM] * (5 + half - 1),
        [out[0], out[1], held, left, right] + got,
    )
    pieces = [agg] + [exchange(agg, "row", s) for s in range(1, row_count)]
    other_g = exchange(near_g, "col", 1)

    size = fin // row_count + -(-classes // (16 * row_count)) * 16 + 16
    back = call(
        functools.partial(back_kernel, row_count, order),
        "back_product",
        [shaped((row_count, tall, nodes), F32)],
        [VMEM] * 4,
        [dense, degree, near_g, other_g],
        scratch=[pltpu.VMEM((tall, rows), BF16)],
    )[0]
    out = call(
        functools.partial(grad_kernel, row_count),
        "gradients",
        [shaped((size, hidden), F32), shaped((tall, columns), BF16), shaped((tall, nodes), F32)]
        + [shaped((size, hidden), BF16)] * (row_count - 1),
        [VMEM] * (2 + row_count + 3),
        [back, own_g] + pieces + [w_first, bias, w2],
        scratch=[pltpu.VMEM((row_count, size, hidden), F32)],
    )
    mine = out[0]
    for s in range(1, row_count):
        mine = mine + exchange(out[2 + s], "row", s).astype(F32)

    send, keep = call(
        second_kernel,
        "second_product",
        [shaped((half, tall, nodes), BF16), shaped((half, tall, nodes), F32)],
        [VMEM, VMEM, VMEM, ANY],
        [dense, out[1], out[2], out[0]],
    )
    out = call(
        functools.partial(core_kernel, half),
        "second_core_sum",
        [shaped((tall, nodes), F32), shaped((size, hidden), BF16)] + [shaped((tall, nodes), BF16)] * (half - 1),
        [VMEM] * 4,
        [keep, exchange(send, "col", 1), mine, exchange(mine, "col", 1)],
    )
    shares = [out[1].astype(F32)] + [exchange(out[1], "col", 2 * s).astype(F32) for s in range(1, half)]
    share = tree_sum(shares).astype(BF16)
    parts = [exchange(out[1 + s], "col", 2 * s) for s in range(1, half)]
    shares = [share] + [exchange(share, "row", s) for s in range(1, row_count)]
    logits, grad_w1, grad_b1, grad_w2, grad_b2 = call(
        functools.partial(last_kernel, row_count, half),
        "results",
        [
            shaped((classes, nodes), BF16),
            shaped((fin, hidden), F32),
            shaped((1, hidden), F32),
            shaped((classes, hidden), F32),
            shaped((1, classes), F32),
        ],
        [VMEM] * (3 + half - 1 + row_count),
        [out[0], degree, b_second[None, :]] + parts + shares,
        scratch=[pltpu.VMEM(((size - fin // row_count - 16) * row_count, hidden), F32)],
    )
    return logits.T, grad_w1, grad_b1[0], grad_w2.T, grad_b2[0]


def solution(mesh):
    return jax.shard_map(
        local,
        mesh=mesh,
        in_specs=(
            P(("row", "col"), None),
            P("row", "col", None, None, None),
            P("row", "col", None),
            P("row", "col", None),
            P("row", "col"),
            P(),
            P(),
            P(),
            P(),
            P(("row", "col"), None),
        ),
        out_specs=(P(("row", "col"), None), P(), P(), P(), P()),
        check_vma=False,
    )
```

```python
import functools
import math

import jax
import jax.numpy as jnp
from jax import lax
from jax.experimental import pallas as pl
from jax.experimental.pallas import tpu as pltpu
from jax.sharding import PartitionSpec as P

BF16 = jnp.bfloat16
F32 = jnp.float32
LANES = 128
GRANT = 820 << 16
VMEM = pl.BlockSpec(memory_space=pltpu.VMEM)
ANY = pl.BlockSpec(memory_space=pl.ANY)
HBM = pl.BlockSpec(memory_space=pltpu.HBM)


def exchange(value, axis, mask):
    count = lax.axis_size(axis)
    return lax.ppermute(value, axis, [(i, i ^ mask) for i in range(count)])


def call(kernel, name, outs, in_specs, args, scratch=(), grant=None):
    size = sum(math.prod(a.shape) * a.dtype.itemsize for a in [*args, *outs])
    grant = min(size + (6 << 20), 60 << 20) if grant is None else grant
    return pl.pallas_call(
        kernel,
        out_shape=tuple(outs),
        in_specs=in_specs,
        out_specs=tuple(VMEM for _ in outs),
        scratch_shapes=scratch,
        compiler_params=pltpu.CompilerParams(vmem_limit_bytes=grant),
        name=name,
    )(*args)


def shaped(shape, dtype):
    return jax.ShapeDtypeStruct(shape, dtype)


def product(left, right, contract=((1,), (0,))):
    return lax.dot_general(left, right, (contract, ((), ())), preferred_element_type=F32)


def split(value):
    high = value.astype(BF16)
    return high, (value - high.astype(F32)).astype(BF16)


def dense_kernel(own, row_hbm, col_hbm, live_hbm, tiles_hbm, features_hbm, g_hbm, next_hbm, *refs):
    dense_ref, held_ref, g_ref, row_ref, col_ref, live_ref, tiles_ref, done = refs
    pairs = (
        (row_hbm, row_ref),
        (col_hbm, col_ref),
        (live_hbm, live_ref),
        (tiles_hbm, tiles_ref),
        (features_hbm, held_ref.at[0]),
        (next_hbm, held_ref.at[1]),
        (g_hbm, g_ref),
    )
    copies = [pltpu.make_async_copy(a, b, done.at[n]) for n, (a, b) in enumerate(pairs)]
    for copy in copies:
        copy.start()
    block = tiles_ref.shape[-1]
    rows, columns = dense_ref.shape
    half = rows // (block * own * 2)
    r, c = lax.axis_index("row"), lax.axis_index("col")
    dense_ref[...] = jnp.zeros_like(dense_ref)
    for copy in copies[:4]:
        copy.wait()

    @pl.loop(0, live_ref[0, 0])
    def _(slot):
        k = row_ref[0, 0, slot]
        j = col_ref[0, 0, slot]
        p = (k // own) ^ c
        at_row = ((p & 1) * half + (p >> 1)) * own + k % own
        at_col = ((j // own) ^ r) * own + j % own
        dense_ref[
            pl.ds(pl.multiple_of(at_row * block, block), block),
            pl.ds(pl.multiple_of(at_col * block, block), block),
        ] = tiles_ref[0, 0, slot]

    for copy in copies[4:]:
        copy.wait()


def first_kernel(spans, dense_ref, g_ref, far_ref, pair_in_ref, *refs):
    pieces, (send_ref, keep_ref, degree_ref, pair_ref, held) = refs[: spans - 2], refs[spans - 2 :]
    pair_ref[0] = g_ref[...]
    pair_ref[1] = far_ref[...]
    nodes = g_ref.shape[1]
    fin = pair_in_ref.shape[2]
    block = LANES
    for s in range(spans):
        held[pl.ds(s * nodes, nodes), :fin] = pair_in_ref[s] if s < 2 else pieces[s - 2][...]
    held[:, fin:] = jnp.ones((held.shape[0], block), BF16)
    half = keep_ref.shape[0] // nodes
    blocks = degree_ref.shape[0]
    line = lax.broadcasted_iota(jnp.int32, (block, block), 0) == lax.broadcasted_iota(jnp.int32, (block, block), 1)

    for s in range(2 * half):
        out = product(dense_ref[pl.ds(s * nodes, nodes), :], held[...])
        if s < half:
            keep_ref[pl.ds(s * nodes, nodes), :] = out[:, :fin]
        else:
            send_ref[pl.ds((s - half) * nodes, nodes), :] = out[:, :fin].astype(BF16)
        for b in range(nodes // block):
            sums = jnp.where(line, out[b * block : (b + 1) * block, fin:], 0.0)
            at = s * (nodes // block) + b
            degree_ref[at : at + 1, :] = jnp.sum(sums, axis=0, keepdims=True)
    high, low = split(degree_ref[...])
    send_ref[pl.ds(half * nodes, blocks), :] = high
    send_ref[pl.ds(half * nodes + blocks, blocks), :] = low


def near_kernel(half, keep_ref, other_ref, part_ref, own_ref, degree_ref, *sends):
    nodes = own_ref.shape[0]
    blocks = part_ref.shape[0]
    tail = other_ref[pl.ds(half * nodes, blocks), :].astype(F32)
    tail = tail + other_ref[pl.ds(half * nodes + blocks, blocks), :].astype(F32)
    degree = part_ref[...] + jnp.concatenate([tail[blocks // 2 :], tail[: blocks // 2]], axis=0)
    degree_ref[...] = degree
    high, low = split(degree)
    own_ref[...] = keep_ref[:nodes, :] + other_ref[:nodes, :].astype(F32)
    for s in range(1, half):
        at = slice(s * nodes, (s + 1) * nodes)
        sends[s - 1][:nodes, :] = (keep_ref[at, :] + other_ref[at, :].astype(F32)).astype(BF16)
        sends[s - 1][nodes : nodes + blocks, :] = high
        sends[s - 1][nodes + blocks :, :] = low


def swapped(value, half, mask):
    own = value.shape[0] // (2 * half)
    order = [h * half + (s ^ mask) for h in range(2) for s in range(half)]
    return jnp.concatenate([value[q * own : (q + 1) * own] for q in order], axis=0)


def agg_kernel(half, near_ref, part_ref, held_ref, left_ref, right_ref, *refs):
    got, (agg_ref, degree_ref, joined_ref) = refs[: half - 1], refs[half - 1 :]
    joined_ref[: half // 2] = left_ref[...]
    joined_ref[half // 2 :] = right_ref[...]
    nodes = held_ref.shape[1]
    block = LANES
    blocks = degree_ref.shape[0]
    total = near_ref[...]
    degree = part_ref[...]
    for s, ref in enumerate(got):
        total = total + ref[:nodes, :].astype(F32)
        tail = ref[nodes : nodes + blocks, :].astype(F32) + ref[nodes + blocks :, :].astype(F32)
        degree = degree + swapped(tail, half, s + 1)
    degree = 1.0 + degree
    degree_ref[...] = degree
    upright = degree.T
    total = total + held_ref[0].astype(F32)
    for b in range(nodes // block):
        at = slice(b * block, (b + 1) * block)
        agg_ref[at, :] = (total[at] / upright[:, b : b + 1]).astype(BF16)


def tree_sum(values):
    while len(values) > 1:
        values = [a + b for a, b in zip(values[::2], values[1::2])]
    return values[0]


def gelu_parts(z):
    scale = 0.7978845608028654
    t = jnp.tanh(scale * (z + 0.044715 * (z * z * z)))
    value = 0.5 * z * (1.0 + t)
    slope = 0.5 * (1.0 + t) + 0.5 * z * (1.0 - t * t) * (scale * (1.0 + 3.0 * 0.044715 * (z * z)))
    return value, slope


def second_kernel(spans, dense_ref, outer_ref, inner_ref, first_ref, after_ref, send_ref, keep_ref, held):
    half, _, nodes = keep_ref.shape
    held[:, :nodes] = outer_ref[:, :nodes]
    held[:, nodes : (spans - 1) * nodes] = inner_ref[...]
    held[:, (spans - 1) * nodes :] = outer_ref[:, nodes:]

    @pl.loop(0, half)
    def _(s):
        at = pl.multiple_of((half + s) * nodes, nodes)
        send_ref[s] = product(held[...], dense_ref[pl.ds(at, nodes), :], ((1,), (1,))).astype(BF16)
        at = pl.multiple_of(s * nodes, nodes)
        keep_ref[s] = product(held[...], dense_ref[pl.ds(at, nodes), :], ((1,), (1,)))

    keep_ref[0] += first_ref[...]


def back_kernel(spans, order, dense_ref, degree_ref, near_ref, other_ref, back_ref, turned):
    _, classes, nodes = near_ref.shape
    tall = turned.shape[0]
    for q in range(2 * len(order)):
        source = near_ref if q < len(order) else other_ref
        degree = jnp.concatenate([degree_ref[2 * q : 2 * q + 1, :], degree_ref[2 * q + 1 : 2 * q + 2, :]], axis=1)
        scaled = source[order.index(q % len(order))].astype(F32) / degree
        if tall > classes:
            scaled = jnp.concatenate([scaled, jnp.zeros((tall - classes, nodes), F32)], axis=0)
        turned[:, q * nodes : (q + 1) * nodes] = scaled.astype(BF16)
    for s in range(spans):
        part = product(turned[...], dense_ref[:, s * nodes : (s + 1) * nodes])
        if s == 0:
            part = part + turned[:, :nodes].astype(F32)
        back_ref[s] = part


def grad_parts(places, back_ref, pieces, w1_ref, b1_ref, w2_ref, hidden_ref, first_ref):
    fin, hidden = w1_ref.shape
    block = LANES
    tall = back_ref.shape[1]
    nodes = pieces[0].shape[0]
    classes = w2_ref.shape[0]
    w2 = jnp.concatenate([w2_ref[...].astype(F32), jnp.zeros((2 * block - classes, hidden), F32)], axis=0).astype(BF16)
    grad_w1 = jnp.zeros((fin, hidden), F32)
    grad_w2 = jnp.zeros((tall, hidden), F32)
    grad_b1 = jnp.zeros((1, hidden), F32)
    for n, s in enumerate(places):
        agg = pieces[n][...]
        value, slope = gelu_parts(product(agg, w1_ref[...]) + b1_ref[...])
        h = value.astype(BF16)
        projected = product(w2, h, ((1,), (1,)))[:tall]
        hidden_ref[:, n * nodes : (n + 1) * nodes] = projected.astype(BF16)
        if s == 0:
            first_ref[...] = projected
        q = back_ref[s]
        high, low = split(q)
        grad_w2 = grad_w2 + product(high, h) + product(low, h)
        high, low = split(jnp.concatenate([q, jnp.zeros((2 * block - tall, nodes), F32)], axis=0).T)
        d_first = (product(high, w2) + product(low, w2)) * slope
        grad_w1 = grad_w1 + product(agg.astype(F32).T.astype(BF16), d_first.astype(BF16))
        grad_b1 = grad_b1 + jnp.sum(d_first, axis=0, keepdims=True)
    return grad_w1, grad_w2, grad_b1


def early_kernel(places, back_ref, own_ref, last_ref, w1_ref, b1_ref, w2_ref, *refs):
    out1_ref, out2_ref, bias_ref, hidden_ref, first_ref = refs
    out1_ref[...], out2_ref[...], bias_ref[...] = grad_parts(
        places, back_ref, (own_ref, last_ref), w1_ref, b1_ref, w2_ref, hidden_ref, first_ref
    )


def grad_kernel(spans, places, back_ref, g_ref, in1_ref, in2_ref, inb_ref, *refs):
    pieces, refs = refs[: len(places)], refs[len(places) :]
    w1_ref, b1_ref, w2_ref, mine_ref, hidden_ref, refs = refs[0], refs[1], refs[2], refs[3], refs[4], refs[5:]
    sends, total = refs[: spans - 1], refs[-1]
    fin = w1_ref.shape[0]
    classes, nodes = g_ref.shape
    tall = back_ref.shape[1]
    rank = lax.axis_index("row")
    parts = grad_parts(places, back_ref, pieces, w1_ref, b1_ref, w2_ref, hidden_ref, None)
    grad_w1, grad_w2, grad_b1 = in1_ref[...] + parts[0], in2_ref[...] + parts[1], inb_ref[...] + parts[2]
    grad_b2 = product(jnp.ones((8, nodes), BF16), g_ref[...], ((1,), (1,)))[:1]
    a = fin // spans
    b = total.shape[1] - a - 16
    total[...] = jnp.zeros_like(total)
    for t in range(spans):
        total[t, :a, :] = grad_w1[t * a : (t + 1) * a]
        have = min(b, tall - t * b)
        if have > 0:
            total[t, a : a + have, :] = grad_w2[t * b : t * b + have]
    total[0, a + b : a + b + 1, :] = grad_b1
    total[0, a + b + 1 : a + b + 2, :classes] = grad_b2
    mine_ref[...] = total[rank]
    for s in range(1, spans):
        sends[s - 1][...] = total[rank ^ s].astype(BF16)


def core_kernel(half, keep_ref, other_ref, mine_ref, far_ref, own_ref, share_ref, *sends):
    share_ref[...] = (mine_ref[...] + far_ref[...]).astype(BF16)
    own_ref[...] = keep_ref[0] + other_ref[0].astype(F32)
    for s in range(1, half):
        sends[s - 1][...] = (keep_ref[s] + other_ref[s].astype(F32)).astype(BF16)


def last_kernel(spans, half, total_ref, degree_ref, bias_ref, *refs):
    parts, refs = refs[: half - 1], refs[half - 1 :]
    got, (logits_ref, w1_ref, b1_ref, w2_ref, b2_ref, tall_ref) = refs[:spans], refs[spans:]
    total = total_ref[...]
    for ref in parts:
        total = total + ref[...].astype(F32)
    nodes = total.shape[1]
    classes = logits_ref.shape[0]
    degree = jnp.concatenate([degree_ref[b : b + 1, :] for b in range(nodes // LANES)], axis=1)
    bias = jnp.concatenate([bias_ref[...], jnp.zeros((1, 2 * LANES - classes), F32)], axis=1)
    bias = jnp.broadcast_to(bias, (8, 2 * LANES)).T
    logits_ref[...] = (total[:classes] / degree + bias[:classes, :1]).astype(BF16)
    fin, hidden = w1_ref.shape
    classes = w2_ref.shape[0]
    a = fin // spans
    b = got[0].shape[0] - a - 16
    for s in range(spans):
        t = lax.axis_index("row") ^ s
        share = got[s][...].astype(F32)
        w1_ref[pl.ds(pl.multiple_of(t * a, a), a), :] = share[:a]
        tall_ref[pl.ds(pl.multiple_of(t * b, b), b), :] = share[a : a + b]

        @pl.when(t == 0)
        def _():
            b1_ref[...] = share[a + b : a + b + 1]
            b2_ref[...] = share[a + b + 1 : a + b + 2, :classes]

    w2_ref[...] = tall_ref[:classes, :]


def local(
    features,
    tiles,
    tile_row,
    tile_col,
    tile_live,
    w_first,
    b_first,
    w_second,
    b_second,
    grad_logits,
):
    row_count = lax.axis_size("row")
    col_count = lax.axis_size("col")
    half = col_count // 2
    nodes, fin = features.shape
    block = tiles.shape[-1]
    own = nodes // block
    hidden = w_first.shape[1]
    classes = w_second.shape[1]
    tall = -(-classes // 16) * 16
    rows, columns = col_count * nodes, row_count * nodes
    blocks = rows // block
    bias = b_first[None, :]
    w2 = w_second.T
    g_own = grad_logits.T

    inputs = [features] + [exchange(features, "row", s) for s in range(1, row_count)]
    far_g = exchange(g_own, "col", half)
    order = [0]
    mask = half
    while mask > 1:
        order = order + [s ^ (mask // 2) for s in order]
        mask //= 2

    whole = rows * columns * 2 <= 4 << 20
    keep_in = pltpu.VMEM if whole else shaped
    dense, held, own_g = call(
        functools.partial(dense_kernel, own),
        "dense_adjacency",
        [
            keep_in((rows, columns), BF16),
            keep_in((2, nodes, fin), BF16),
            keep_in(g_own.shape, BF16),
        ],
        [HBM] * 7,
        [tile_row, tile_col, tile_live, tiles, features, g_own, inputs[1]],
        scratch=[
            pltpu.SMEM(tile_row.shape, jnp.int32),
            pltpu.SMEM(tile_col.shape, jnp.int32),
            pltpu.SMEM(tile_live.shape, jnp.int32),
            pltpu.VMEM(tiles.shape, BF16),
            pltpu.SemaphoreType.DMA((7,)),
        ],
        grant=GRANT if whole else 60 << 20,
    )
    send, keep, degree, left = call(
        functools.partial(first_kernel, row_count),
        "first_product",
        [
            shaped((rows // 2 + 2 * blocks, fin), BF16),
            shaped((rows // 2, fin), F32),
            shaped((blocks, block), F32),
            shaped((2, classes, nodes), BF16),
        ],
        [VMEM] * (2 + row_count),
        [dense, own_g, far_g, held] + inputs[2:],
        scratch=[pltpu.VMEM((columns, fin + LANES), BF16)],
    )
    other = exchange(send, "col", 1)
    mask = half // 2
    while mask > 2:
        left = jnp.concatenate([left, exchange(left, "col", mask)], axis=0)
        mask //= 2
    right = exchange(left, "col", mask)
    out = call(
        functools.partial(near_kernel, half),
        "first_core_sum",
        [shaped((nodes, fin), F32), shaped((blocks, block), F32)]
        + [shaped((nodes + 2 * blocks, fin), BF16)] * (half - 1),
        [VMEM] * 3,
        [keep, other, degree],
    )
    got = [exchange(out[1 + s], "col", 2 * s) for s in range(1, half)]
    agg, degree, near_g = call(
        functools.partial(agg_kernel, half),
        "first_aggregate",
        [shaped((nodes, fin), BF16), shaped((blocks, block), F32), shaped((half, classes, nodes), BF16)],
        [VMEM] * (5 + half - 1),
        [out[0], out[1], held, left, right] + got,
    )
    pieces = [agg] + [exchange(agg, "row", s) for s in range(1, row_count)]
    other_g = exchange(near_g, "col", 1)

    size = fin // row_count + -(-classes // (16 * row_count)) * 16 + 16
    back = call(
        functools.partial(back_kernel, row_count, order),
        "back_product",
        [shaped((row_count, tall, nodes), F32)],
        [VMEM] * 4,
        [dense, degree, near_g, other_g],
        scratch=[pltpu.VMEM((tall, rows), BF16)],
    )[0]
    outer = [0, row_count - 1]
    inner = list(range(1, row_count - 1))
    early = call(
        functools.partial(early_kernel, outer),
        "gradients_early",
        [
            shaped((fin, hidden), F32),
            shaped((tall, hidden), F32),
            shaped((1, hidden), F32),
            shaped((tall, 2 * nodes), BF16),
            shaped((tall, nodes), F32),
        ],
        [VMEM] * 6,
        [back, pieces[0], pieces[-1], w_first, bias, w2],
    )
    out = call(
        functools.partial(grad_kernel, row_count, inner),
        "gradients",
        [shaped((size, hidden), F32), shaped((tall, columns - 2 * nodes), BF16)]
        + [shaped((size, hidden), BF16)] * (row_count - 1),
        [VMEM] * (5 + row_count - 2 + 3),
        [back, own_g, *early[:3]] + pieces[1:-1] + [w_first, bias, w2],
        scratch=[pltpu.VMEM((row_count, size, hidden), F32)],
    )
    mine = out[0]
    for s in range(1, row_count):
        mine = mine + exchange(out[1 + s], "row", s).astype(F32)

    send, keep = call(
        functools.partial(second_kernel, row_count),
        "second_product",
        [shaped((half, tall, nodes), BF16), shaped((half, tall, nodes), F32)],
        [VMEM, VMEM, VMEM, VMEM, ANY],
        [dense, early[3], out[1], early[4], out[0]],
        scratch=[pltpu.VMEM((tall, columns), BF16)],
    )
    out = call(
        functools.partial(core_kernel, half),
        "second_core_sum",
        [shaped((tall, nodes), F32), shaped((size, hidden), BF16)] + [shaped((tall, nodes), BF16)] * (half - 1),
        [VMEM] * 4,
        [keep, exchange(send, "col", 1), mine, exchange(mine, "col", 1)],
    )
    shares = [out[1].astype(F32)] + [exchange(out[1], "col", 2 * s).astype(F32) for s in range(1, half)]
    share = tree_sum(shares).astype(BF16)
    parts = [exchange(out[1 + s], "col", 2 * s) for s in range(1, half)]
    shares = [share] + [exchange(share, "row", s) for s in range(1, row_count)]
    logits, grad_w1, grad_b1, grad_w2, grad_b2 = call(
        functools.partial(last_kernel, row_count, half),
        "results",
        [
            shaped((classes, nodes), BF16),
            shaped((fin, hidden), F32),
            shaped((1, hidden), F32),
            shaped((classes, hidden), F32),
            shaped((1, classes), F32),
        ],
        [VMEM] * (3 + half - 1 + row_count),
        [out[0], degree, b_second[None, :]] + parts + shares,
        scratch=[pltpu.VMEM(((size - fin // row_count - 16) * row_count, hidden), F32)],
    )
    return logits.T, grad_w1, grad_b1[0], grad_w2.T, grad_b2[0]


def solution(mesh):
    return jax.shard_map(
        local,
        mesh=mesh,
        in_specs=(
            P(("row", "col"), None),
            P("row", "col", None, None, None),
            P("row", "col", None),
            P("row", "col", None),
            P("row", "col"),
            P(),
            P(),
            P(),
            P(),
            P(("row", "col"), None),
        ),
        out_specs=(P(("row", "col"), None), P(), P(), P(), P()),
        check_vma=False,
    )
```

```python
import functools
import math

import jax
import jax.numpy as jnp
from jax import lax
from jax.experimental import pallas as pl
from jax.experimental.pallas import tpu as pltpu
from jax.sharding import PartitionSpec as P

BF16 = jnp.bfloat16
F32 = jnp.float32
LANES = 128
GRANT = 820 << 16
VMEM = pl.BlockSpec(memory_space=pltpu.VMEM)
ANY = pl.BlockSpec(memory_space=pl.ANY)
HBM = pl.BlockSpec(memory_space=pltpu.HBM)


def exchange(value, axis, mask):
    count = lax.axis_size(axis)
    return lax.ppermute(value, axis, [(i, i ^ mask) for i in range(count)])


def call(kernel, name, outs, in_specs, args, scratch=(), grant=None):
    size = sum(math.prod(a.shape) * a.dtype.itemsize for a in [*args, *outs])
    grant = min(size + (6 << 20), 60 << 20) if grant is None else grant
    return pl.pallas_call(
        kernel,
        out_shape=tuple(outs),
        in_specs=in_specs,
        out_specs=tuple(VMEM for _ in outs),
        scratch_shapes=scratch,
        compiler_params=pltpu.CompilerParams(vmem_limit_bytes=grant),
        name=name,
    )(*args)


def shaped(shape, dtype):
    return jax.ShapeDtypeStruct(shape, dtype)


def product(left, right, contract=((1,), (0,))):
    return lax.dot_general(left, right, (contract, ((), ())), preferred_element_type=F32)


def split(value):
    high = value.astype(BF16)
    return high, (value - high.astype(F32)).astype(BF16)


def dense_kernel(own, row_hbm, col_hbm, live_hbm, tiles_hbm, features_hbm, g_hbm, *refs):
    dense_ref, held_ref, g_ref, row_ref, col_ref, live_ref, tiles_ref, done = refs
    pairs = (
        (row_hbm, row_ref),
        (col_hbm, col_ref),
        (live_hbm, live_ref),
        (tiles_hbm, tiles_ref),
        (features_hbm, held_ref.at[0]),
        (g_hbm, g_ref),
    )
    copies = [pltpu.make_async_copy(a, b, done.at[n]) for n, (a, b) in enumerate(pairs)]
    for copy in copies:
        copy.start()
    block = tiles_ref.shape[-1]
    rows, columns = dense_ref.shape
    half = rows // (block * own * 2)
    r, c = lax.axis_index("row"), lax.axis_index("col")
    dense_ref[...] = jnp.zeros_like(dense_ref)
    for copy in copies[:4]:
        copy.wait()

    @pl.loop(0, live_ref[0, 0])
    def _(slot):
        k = row_ref[0, 0, slot]
        j = col_ref[0, 0, slot]
        p = (k // own) ^ c
        at_row = ((p & 1) * half + (p >> 1)) * own + k % own
        at_col = ((j // own) ^ r) * own + j % own
        dense_ref[
            pl.ds(pl.multiple_of(at_row * block, block), block),
            pl.ds(pl.multiple_of(at_col * block, block), block),
        ] = tiles_ref[0, 0, slot]

    for copy in copies[4:]:
        copy.wait()


def first_kernel(spans, dense_ref, g_ref, far_ref, pair_in_ref, *refs):
    pieces, (send_ref, keep_ref, degree_ref, pair_ref, held) = refs[: spans - 1], refs[spans - 1 :]
    pair_ref[0] = g_ref[...]
    pair_ref[1] = far_ref[...]
    nodes = g_ref.shape[1]
    fin = pair_in_ref.shape[2]
    block = LANES
    for s in range(spans):
        held[pl.ds(s * nodes, nodes), :fin] = pair_in_ref[0] if s == 0 else pieces[s - 1][...]
    held[:, fin:] = jnp.ones((held.shape[0], block), BF16)
    half = keep_ref.shape[0] // nodes
    blocks = degree_ref.shape[0]
    line = lax.broadcasted_iota(jnp.int32, (block, block), 0) == lax.broadcasted_iota(jnp.int32, (block, block), 1)

    for s in range(2 * half):
        out = product(dense_ref[pl.ds(s * nodes, nodes), :], held[...])
        if s < half:
            keep_ref[pl.ds(s * nodes, nodes), :] = out[:, :fin]
        else:
            send_ref[pl.ds((s - half) * nodes, nodes), :] = out[:, :fin].astype(BF16)
        for b in range(nodes // block):
            sums = jnp.where(line, out[b * block : (b + 1) * block, fin:], 0.0)
            at = s * (nodes // block) + b
            degree_ref[at : at + 1, :] = jnp.sum(sums, axis=0, keepdims=True)
    high, low = split(degree_ref[...])
    send_ref[pl.ds(half * nodes, blocks), :] = high
    send_ref[pl.ds(half * nodes + blocks, blocks), :] = low


def near_kernel(half, keep_ref, other_ref, part_ref, own_ref, degree_ref, *sends):
    nodes = own_ref.shape[0]
    blocks = part_ref.shape[0]
    tail = other_ref[pl.ds(half * nodes, blocks), :].astype(F32)
    tail = tail + other_ref[pl.ds(half * nodes + blocks, blocks), :].astype(F32)
    degree = part_ref[...] + jnp.concatenate([tail[blocks // 2 :], tail[: blocks // 2]], axis=0)
    degree_ref[...] = degree
    high, low = split(degree)
    own_ref[...] = keep_ref[:nodes, :] + other_ref[:nodes, :].astype(F32)
    for s in range(1, half):
        at = slice(s * nodes, (s + 1) * nodes)
        sends[s - 1][:nodes, :] = (keep_ref[at, :] + other_ref[at, :].astype(F32)).astype(BF16)
        sends[s - 1][nodes : nodes + blocks, :] = high
        sends[s - 1][nodes + blocks :, :] = low


def swapped(value, half, mask):
    own = value.shape[0] // (2 * half)
    order = [h * half + (s ^ mask) for h in range(2) for s in range(half)]
    return jnp.concatenate([value[q * own : (q + 1) * own] for q in order], axis=0)


def agg_kernel(half, near_ref, part_ref, held_ref, left_ref, right_ref, *refs):
    got, (agg_ref, degree_ref, joined_ref) = refs[: half - 1], refs[half - 1 :]
    joined_ref[: half // 2] = left_ref[...]
    joined_ref[half // 2 :] = right_ref[...]
    nodes = held_ref.shape[1]
    block = LANES
    blocks = degree_ref.shape[0]
    total = near_ref[...]
    degree = part_ref[...]
    for s, ref in enumerate(got):
        total = total + ref[:nodes, :].astype(F32)
        tail = ref[nodes : nodes + blocks, :].astype(F32) + ref[nodes + blocks :, :].astype(F32)
        degree = degree + swapped(tail, half, s + 1)
    degree = 1.0 + degree
    degree_ref[...] = degree
    upright = degree.T
    total = total + held_ref[0].astype(F32)
    for b in range(nodes // block):
        at = slice(b * block, (b + 1) * block)
        agg_ref[at, :] = (total[at] / upright[:, b : b + 1]).astype(BF16)


def tree_sum(values):
    while len(values) > 1:
        values = [a + b for a, b in zip(values[::2], values[1::2])]
    return values[0]


def gelu_parts(z):
    scale = 0.7978845608028654
    t = jnp.tanh(scale * (z + 0.044715 * (z * z * z)))
    value = 0.5 * z * (1.0 + t)
    slope = 0.5 * (1.0 + t) + 0.5 * z * (1.0 - t * t) * (scale * (1.0 + 3.0 * 0.044715 * (z * z)))
    return value, slope


def second_kernel(spans, dense_ref, outer_ref, inner_ref, first_ref, after_ref, send_ref, keep_ref, held):
    half, _, nodes = keep_ref.shape
    held[:, :nodes] = outer_ref[:, :nodes]
    held[:, nodes : (spans - 1) * nodes] = inner_ref[...]
    held[:, (spans - 1) * nodes :] = outer_ref[:, nodes:]

    @pl.loop(0, half)
    def _(s):
        at = pl.multiple_of((half + s) * nodes, nodes)
        send_ref[s] = product(held[...], dense_ref[pl.ds(at, nodes), :], ((1,), (1,))).astype(BF16)
        at = pl.multiple_of(s * nodes, nodes)
        keep_ref[s] = product(held[...], dense_ref[pl.ds(at, nodes), :], ((1,), (1,)))

    keep_ref[0] += first_ref[...]


def back_kernel(spans, order, dense_ref, degree_ref, near_ref, other_ref, back_ref, turned):
    _, classes, nodes = near_ref.shape
    tall = turned.shape[0]
    for q in range(2 * len(order)):
        source = near_ref if q < len(order) else other_ref
        degree = jnp.concatenate([degree_ref[2 * q : 2 * q + 1, :], degree_ref[2 * q + 1 : 2 * q + 2, :]], axis=1)
        scaled = source[order.index(q % len(order))].astype(F32) / degree
        if tall > classes:
            scaled = jnp.concatenate([scaled, jnp.zeros((tall - classes, nodes), F32)], axis=0)
        turned[:, q * nodes : (q + 1) * nodes] = scaled.astype(BF16)
    for s in range(spans):
        part = product(turned[...], dense_ref[:, s * nodes : (s + 1) * nodes])
        if s == 0:
            part = part + turned[:, :nodes].astype(F32)
        back_ref[s] = part


def grad_parts(places, back_ref, pieces, w1_ref, b1_ref, w2_ref, hidden_ref, first_ref):
    fin, hidden = w1_ref.shape
    block = LANES
    tall = back_ref.shape[1]
    nodes = pieces[0].shape[0]
    classes = w2_ref.shape[0]
    w2 = jnp.concatenate([w2_ref[...].astype(F32), jnp.zeros((2 * block - classes, hidden), F32)], axis=0).astype(BF16)
    grad_w1 = jnp.zeros((fin, hidden), F32)
    grad_w2 = jnp.zeros((tall, hidden), F32)
    grad_b1 = jnp.zeros((1, hidden), F32)
    for n, s in enumerate(places):
        agg = pieces[n][...]
        value, slope = gelu_parts(product(agg, w1_ref[...]) + b1_ref[...])
        h = value.astype(BF16)
        projected = product(w2, h, ((1,), (1,)))[:tall]
        hidden_ref[:, n * nodes : (n + 1) * nodes] = projected.astype(BF16)
        if s == 0:
            first_ref[...] = projected
        q = back_ref[s]
        high, low = split(q)
        grad_w2 = grad_w2 + product(high, h) + product(low, h)
        high, low = split(jnp.concatenate([q, jnp.zeros((2 * block - tall, nodes), F32)], axis=0).T)
        d_first = (product(high, w2) + product(low, w2)) * slope
        grad_w1 = grad_w1 + product(agg.astype(F32).T.astype(BF16), d_first.astype(BF16))
        grad_b1 = grad_b1 + jnp.sum(d_first, axis=0, keepdims=True)
    return grad_w1, grad_w2, grad_b1


def early_kernel(places, back_ref, own_ref, last_ref, w1_ref, b1_ref, w2_ref, *refs):
    out1_ref, out2_ref, bias_ref, hidden_ref, first_ref = refs
    out1_ref[...], out2_ref[...], bias_ref[...] = grad_parts(
        places, back_ref, (own_ref, last_ref), w1_ref, b1_ref, w2_ref, hidden_ref, first_ref
    )


def grad_kernel(spans, places, back_ref, g_ref, in1_ref, in2_ref, inb_ref, *refs):
    pieces, refs = refs[: len(places)], refs[len(places) :]
    w1_ref, b1_ref, w2_ref, mine_ref, hidden_ref, refs = refs[0], refs[1], refs[2], refs[3], refs[4], refs[5:]
    sends, total = refs[: spans - 1], refs[-1]
    fin = w1_ref.shape[0]
    classes, nodes = g_ref.shape
    tall = back_ref.shape[1]
    rank = lax.axis_index("row")
    parts = grad_parts(places, back_ref, pieces, w1_ref, b1_ref, w2_ref, hidden_ref, None)
    grad_w1, grad_w2, grad_b1 = in1_ref[...] + parts[0], in2_ref[...] + parts[1], inb_ref[...] + parts[2]
    grad_b2 = product(jnp.ones((8, nodes), BF16), g_ref[...], ((1,), (1,)))[:1]
    a = fin // spans
    b = total.shape[1] - a - 16
    total[...] = jnp.zeros_like(total)
    for t in range(spans):
        total[t, :a, :] = grad_w1[t * a : (t + 1) * a]
        have = min(b, tall - t * b)
        if have > 0:
            total[t, a : a + have, :] = grad_w2[t * b : t * b + have]
    total[0, a + b : a + b + 1, :] = grad_b1
    total[0, a + b + 1 : a + b + 2, :classes] = grad_b2
    mine_ref[...] = total[rank]
    for s in range(1, spans):
        sends[s - 1][...] = total[rank ^ s].astype(BF16)


def core_kernel(half, keep_ref, other_ref, mine_ref, far_ref, own_ref, share_ref, *sends):
    share_ref[...] = (mine_ref[...] + far_ref[...]).astype(BF16)
    own_ref[...] = keep_ref[0] + other_ref[0].astype(F32)
    for s in range(1, half):
        sends[s - 1][...] = (keep_ref[s] + other_ref[s].astype(F32)).astype(BF16)


def last_kernel(spans, half, total_ref, degree_ref, bias_ref, *refs):
    parts, refs = refs[: half - 1], refs[half - 1 :]
    got, (logits_ref, w1_ref, b1_ref, w2_ref, b2_ref, tall_ref) = refs[:spans], refs[spans:]
    total = total_ref[...]
    for ref in parts:
        total = total + ref[...].astype(F32)
    nodes = total.shape[1]
    classes = logits_ref.shape[0]
    degree = jnp.concatenate([degree_ref[b : b + 1, :] for b in range(nodes // LANES)], axis=1)
    bias = jnp.concatenate([bias_ref[...], jnp.zeros((1, 2 * LANES - classes), F32)], axis=1)
    bias = jnp.broadcast_to(bias, (8, 2 * LANES)).T
    logits_ref[...] = (total[:classes] / degree + bias[:classes, :1]).astype(BF16)
    fin, hidden = w1_ref.shape
    classes = w2_ref.shape[0]
    a = fin // spans
    b = got[0].shape[0] - a - 16
    for s in range(spans):
        t = lax.axis_index("row") ^ s
        share = got[s][...].astype(F32)
        w1_ref[pl.ds(pl.multiple_of(t * a, a), a), :] = share[:a]
        tall_ref[pl.ds(pl.multiple_of(t * b, b), b), :] = share[a : a + b]

        @pl.when(t == 0)
        def _():
            b1_ref[...] = share[a + b : a + b + 1]
            b2_ref[...] = share[a + b + 1 : a + b + 2, :classes]

    w2_ref[...] = tall_ref[:classes, :]


def local(
    features,
    tiles,
    tile_row,
    tile_col,
    tile_live,
    w_first,
    b_first,
    w_second,
    b_second,
    grad_logits,
):
    row_count = lax.axis_size("row")
    col_count = lax.axis_size("col")
    half = col_count // 2
    nodes, fin = features.shape
    block = tiles.shape[-1]
    own = nodes // block
    hidden = w_first.shape[1]
    classes = w_second.shape[1]
    tall = -(-classes // 16) * 16
    rows, columns = col_count * nodes, row_count * nodes
    blocks = rows // block
    bias = b_first[None, :]
    w2 = w_second.T
    g_own = grad_logits.T

    inputs = [features] + [exchange(features, "row", s) for s in range(1, row_count)]
    far_g = exchange(g_own, "col", half)
    order = [0]
    mask = half
    while mask > 1:
        order = order + [s ^ (mask // 2) for s in order]
        mask //= 2

    whole = rows * columns * 2 <= 4 << 20
    keep_in = pltpu.VMEM if whole else shaped
    dense, held, own_g = call(
        functools.partial(dense_kernel, own),
        "dense_adjacency",
        [
            keep_in((rows, columns), BF16),
            keep_in((1, nodes, fin), BF16),
            keep_in(g_own.shape, BF16),
        ],
        [HBM] * 6,
        [tile_row, tile_col, tile_live, tiles, features, g_own],
        scratch=[
            pltpu.SMEM(tile_row.shape, jnp.int32),
            pltpu.SMEM(tile_col.shape, jnp.int32),
            pltpu.SMEM(tile_live.shape, jnp.int32),
            pltpu.VMEM(tiles.shape, BF16),
            pltpu.SemaphoreType.DMA((6,)),
        ],
        grant=GRANT if whole else 60 << 20,
    )
    send, keep, degree, left = call(
        functools.partial(first_kernel, row_count),
        "first_product",
        [
            shaped((rows // 2 + 2 * blocks, fin), BF16),
            shaped((rows // 2, fin), F32),
            shaped((blocks, block), F32),
            shaped((2, classes, nodes), BF16),
        ],
        [VMEM] * (3 + row_count),
        [dense, own_g, far_g, held] + inputs[1:],
        scratch=[pltpu.VMEM((columns, fin + LANES), BF16)],
    )
    other = exchange(send, "col", 1)
    mask = half // 2
    while mask > 2:
        left = jnp.concatenate([left, exchange(left, "col", mask)], axis=0)
        mask //= 2
    right = exchange(left, "col", mask)
    out = call(
        functools.partial(near_kernel, half),
        "first_core_sum",
        [shaped((nodes, fin), F32), shaped((blocks, block), F32)]
        + [shaped((nodes + 2 * blocks, fin), BF16)] * (half - 1),
        [VMEM] * 3,
        [keep, other, degree],
    )
    got = [exchange(out[1 + s], "col", 2 * s) for s in range(1, half)]
    agg, degree, near_g = call(
        functools.partial(agg_kernel, half),
        "first_aggregate",
        [shaped((nodes, fin), BF16), shaped((blocks, block), F32), shaped((half, classes, nodes), BF16)],
        [VMEM] * (5 + half - 1),
        [out[0], out[1], held, left, right] + got,
    )
    pieces = [agg] + [exchange(agg, "row", s) for s in range(1, row_count)]
    other_g = exchange(near_g, "col", 1)

    size = fin // row_count + -(-classes // (16 * row_count)) * 16 + 16
    back = call(
        functools.partial(back_kernel, row_count, order),
        "back_product",
        [shaped((row_count, tall, nodes), F32)],
        [VMEM] * 4,
        [dense, degree, near_g, other_g],
        scratch=[pltpu.VMEM((tall, rows), BF16)],
    )[0]
    outer = [0, row_count - 1]
    inner = list(range(1, row_count - 1))
    early = call(
        functools.partial(early_kernel, outer),
        "gradients_early",
        [
            shaped((fin, hidden), F32),
            shaped((tall, hidden), F32),
            shaped((1, hidden), F32),
            shaped((tall, 2 * nodes), BF16),
            shaped((tall, nodes), F32),
        ],
        [VMEM] * 6,
        [back, pieces[0], pieces[-1], w_first, bias, w2],
    )
    out = call(
        functools.partial(grad_kernel, row_count, inner),
        "gradients",
        [shaped((size, hidden), F32), shaped((tall, columns - 2 * nodes), BF16)]
        + [shaped((size, hidden), BF16)] * (row_count - 1),
        [VMEM] * (5 + row_count - 2 + 3),
        [back, own_g, *early[:3]] + pieces[1:-1] + [w_first, bias, w2],
        scratch=[pltpu.VMEM((row_count, size, hidden), F32)],
    )
    mine = out[0]
    for s in range(1, row_count):
        mine = mine + exchange(out[1 + s], "row", s).astype(F32)

    send, keep = call(
        functools.partial(second_kernel, row_count),
        "second_product",
        [shaped((half, tall, nodes), BF16), shaped((half, tall, nodes), F32)],
        [VMEM, VMEM, VMEM, VMEM, ANY],
        [dense, early[3], out[1], early[4], out[0]],
        scratch=[pltpu.VMEM((tall, columns), BF16)],
    )
    out = call(
        functools.partial(core_kernel, half),
        "second_core_sum",
        [shaped((tall, nodes), F32), shaped((size, hidden), BF16)] + [shaped((tall, nodes), BF16)] * (half - 1),
        [VMEM] * 4,
        [keep, exchange(send, "col", 1), mine, exchange(mine, "col", 1)],
    )
    shares = [out[1].astype(F32)] + [exchange(out[1], "col", 2 * s).astype(F32) for s in range(1, half)]
    share = tree_sum(shares).astype(BF16)
    parts = [exchange(out[1 + s], "col", 2 * s) for s in range(1, half)]
    shares = [share] + [exchange(share, "row", s) for s in range(1, row_count)]
    logits, grad_w1, grad_b1, grad_w2, grad_b2 = call(
        functools.partial(last_kernel, row_count, half),
        "results",
        [
            shaped((classes, nodes), BF16),
            shaped((fin, hidden), F32),
            shaped((1, hidden), F32),
            shaped((classes, hidden), F32),
            shaped((1, classes), F32),
        ],
        [VMEM] * (3 + half - 1 + row_count),
        [out[0], degree, b_second[None, :]] + parts + shares,
        scratch=[pltpu.VMEM(((size - fin // row_count - 16) * row_count, hidden), F32)],
    )
    return logits.T, grad_w1, grad_b1[0], grad_w2.T, grad_b2[0]


def solution(mesh):
    return jax.shard_map(
        local,
        mesh=mesh,
        in_specs=(
            P(("row", "col"), None),
            P("row", "col", None, None, None),
            P("row", "col", None),
            P("row", "col", None),
            P("row", "col"),
            P(),
            P(),
            P(),
            P(),
            P(("row", "col"), None),
        ),
        out_specs=(P(("row", "col"), None), P(), P(), P(), P()),
        check_vma=False,
    )
```
